256 devices in a mesh: grp: 8 (over y, x_lo), curve: 32 (over z, x_hi, core).
Axes of the slice: x: 4 (x_hi: 2, x_lo: 2; x = x_hi * 2 + x_lo), y: 4, z: 8, core: 2. Of those that a mesh axis runs over, the one named last changes fastest.
Arguments:
- features: bfloat16 [1024, 8, 8, 512], P(('grp', 'curve')), may hold values from -6 to 6
- block_loads: int32 [256], P(('grp', 'curve')), may hold values from 1 to 4
- swap_counts: int32 [8, 2, 32], P('grp'), may hold values from -1 to 1, as said below
- neighbours: int32 [1024, 6], P(('grp', 'curve')), may hold values from -1 to 19, as said below
- occupancy: int32 [1024, 512], P(('grp', 'curve')), may hold values 0 or 1
- conv_weights: bfloat16 [2, 27, 64, 64], replicated, may hold values from -0.15625 to 0.15625
- norm_gains: float32 [2, 64], replicated, may hold values from 0.25 to 1.75
Outputs:
- layer_output: bfloat16 [1024, 8, 8, 512], P(('grp', 'curve'))
The draws below stay inside these ranges and needn't reach their ends.
Inputs may be any that keep to these rules, and one draw needn't show every extreme that they name: `swap_counts`: Section-0 entries at odd owners are 0; the section-1 entry of owner 32 - 1 is 0; in each section an owner gives at most its live blocks in all, and every load stays within 0 to 4. `neighbours`: encoded as source * 4 + slot with source 0 to 4; a named slot is live after rebalancing at that source, which exists on the mesh; dead slots list -1 on every face. Of one owner's entries, at most 4 name any one of the sources 1 to 4, and some owner names exactly 4 from each of two sources.
All inputs are finite; a program needn't handle non-finite values. No bound on the sum of `occupancy` on one device may be relied on, other than what follows from the above.
Results may differ from the reference program's by a relative error of at most 0.0049.
Values may be sent and summed in bfloat16 or wider, within the bound.
A program may use at most 128 MiB of HBM per device.

```python
import jax
import jax.numpy as jnp
from jax import lax

CH = 64
CAP = 4
LAYERS = 2
MOVE = 1
REQUESTS = 4
SLOTS = 1024
N_GRP = 8
N_CURVE = 32


def pinned_owners():
    half = N_CURVE // 2
    return [(0, 0, CAP), (0, 1, 1), (0, half - 2, CAP), (0, half - 1, 1), (0, N_CURVE - 2, CAP), (0, N_CURVE - 1, 1), (1, half - 1, CAP), (1, half, 1), (1, 0, 1), (1, 1, CAP), (1, N_CURVE - 2, 1), (1, N_CURVE - 1, CAP), (2, half - 1, 1), (2, half, CAP), (3, half, 1), (3, half + 1, CAP)]


def balanced_loads(key):
    key = jax.random.fold_in(key, 17)
    drawn = jax.random.randint(key, (N_GRP, N_CURVE), 1, CAP + 1)
    pinned = jnp.zeros((N_GRP, N_CURVE), jnp.int32)
    for group_no, owner_no, load_value in pinned_owners():
        drawn = drawn.at[group_no, owner_no].set(load_value)
        pinned = pinned.at[group_no, owner_no].set(1)
    return (drawn.astype(jnp.int32), pinned)


def pair_flows(loaded):
    before, pinned = loaded
    difference = before[:, 0::2] - before[:, 1::2]
    first_sizes = jnp.sign(difference) * jnp.minimum(MOVE, jnp.abs(difference) // 2)
    touched = pinned[:, 0::2] + pinned[:, 1::2] > 0
    first_sizes = jnp.where(touched, 0, first_sizes)
    first_counts = jnp.zeros_like(before).at[:, 0::2].set(first_sizes)
    middle = before.at[:, 0::2].add(-first_sizes).at[:, 1::2].add(first_sizes)
    chain_difference = middle[:, :N_CURVE - 1] - middle[:, 1:]
    chain_sizes = jnp.sign(chain_difference) * jnp.minimum(MOVE, jnp.abs(chain_difference) // 2)
    second_counts = jnp.zeros_like(before).at[:, :N_CURVE - 1].set(chain_sizes)
    settled = middle.at[:, :N_CURVE - 1].add(-chain_sizes).at[:, 1:].add(chain_sizes)
    return (first_counts, second_counts, settled)


def draw_block_loads(key, part):
    drawn = balanced_loads(key)[0]
    return drawn.reshape(-1).astype(jnp.int32)


def draw_swap_counts(key, part):
    first_counts, second_counts, settled = pair_flows(balanced_loads(key))
    return jnp.stack([first_counts, second_counts], axis=1).astype(jnp.int32)


def draw_neighbours(key, part):
    settled = pair_flows(balanced_loads(key))[2].reshape(-1)
    key = jax.random.fold_in(key, 7)
    kind_key, slot_key, miss_key = jax.random.split(key, 3)
    slot_ids = jnp.arange(SLOTS)
    device = slot_ids // CAP
    within = slot_ids % CAP
    group_col = (device // N_CURVE)[:, None]
    position_col = (device % N_CURVE)[:, None]
    kind_drawn = jax.random.randint(kind_key, (SLOTS, 6), 0, 8)
    source = jnp.array([0, 0, 0, 1, 2, 3, 4, 1], jnp.int32)[kind_drawn]
    blocked = (source == 1) & (position_col == 0) | (source == 2) & (position_col == N_CURVE - 1)
    blocked = blocked | (source == 3) & (group_col == 0) | (source == 4) & (group_col == N_GRP - 1)
    source = jnp.where(blocked, 0, source)
    missing = jax.random.randint(miss_key, (SLOTS, 6), 0, 4) == 0
    is_dead = jnp.broadcast_to((within >= settled[device])[:, None], (SLOTS, 6))
    source = jnp.where(missing | is_dead, -1, source)
    flat = source.reshape(N_GRP * N_CURVE, CAP * 6)
    for source_no in range(1, 5):
        marked = flat == source_no
        counted = jnp.cumsum(marked.astype(jnp.int32), axis=1)
        flat = jnp.where(marked & (counted > REQUESTS), 0, flat)
    entry = jnp.arange(CAP * 6)
    forced = jnp.where(entry < REQUESTS, 2, 4)
    first_row = flat[0]
    first_row = jnp.where((first_row == 2) | (first_row == 4), 0, first_row)
    first_row = jnp.where(entry < 2 * REQUESTS, forced, first_row)
    flat = flat.at[0].set(first_row)
    source = flat.reshape(SLOTS, 6)
    is_live = source >= 0
    source = jnp.maximum(source, 0)
    step_group = jnp.array([0, 0, 0, -1, 1], jnp.int32)[source]
    step_owner = jnp.array([0, -1, 1, 0, 0], jnp.int32)[source]
    target = (group_col + step_group) * N_CURVE + position_col + step_owner
    raw_draw = jax.random.randint(slot_key, (SLOTS, 6), 0, 1 << 20)
    slot_drawn = raw_draw % settled[target]
    encoded = source * CAP + slot_drawn
    return jnp.where(is_live, encoded, -1).astype(jnp.int32)


def with_ends(values, key, low, top_value):
    dims = values.shape
    place = [jax.random.randint(jax.random.fold_in(key, axis), (), 0, dims[axis]) for axis in range(len(dims))]
    values = values.at[tuple(place)].set(low)
    longest = dims.index(max(dims))
    place[longest] = (place[longest] + 1) % dims[longest]
    return values.at[tuple(place)].set(top_value)


def block_scale(key, shape, cuts, smallest, high):
    gain = 1.0
    for dim, blocks in cuts:
        draws = jax.random.uniform(jax.random.fold_in(jax.random.fold_in(key, 6), dim), (blocks,), jnp.float32, smallest / len(cuts), high / len(cuts))
        gain = gain * jnp.repeat(jnp.exp(draws), shape[dim] // blocks).reshape((-1,) + (1,) * (len(shape) - 1 - dim))
    return gain


def scatter_about(rng, dims, spread, reach, shards=(), kind=jnp.bfloat16):
    values = jax.random.normal(rng, dims, jnp.float32) * spread
    if len(shards) > 0:
        values = block_scale(rng, dims, shards, -0.22, 0.18) * values
    return jnp.clip(values, min=-reach, max=reach).astype(kind)


def setup_inputs(seed: int = 0) -> dict:
    splits = jax.random.split(jax.random.key(seed), 8)
    features = scatter_about(splits[0], (SLOTS, 8, 8, 8 * CH), 1.0, 6.0, ((0, 256),))
    block_loads = draw_block_loads(jax.random.fold_in(splits[7], 71), 0)
    swap_counts = draw_swap_counts(jax.random.fold_in(splits[7], 71), 0)
    neighbours = draw_neighbours(jax.random.fold_in(splits[7], 71), 0)
    occupancy = with_ends((jax.random.randint(splits[4], (SLOTS, 512), 0, 5) < 3).astype(jnp.int32), jax.random.fold_in(splits[4], 1), 0, 1)
    conv_weights = scatter_about(splits[5], (LAYERS, 27, CH, CH), (27 * CH) ** -0.5, 0.15625)
    norm_gains = jnp.clip(1.0 + 0.15 * jax.random.normal(splits[6], (LAYERS, CH), jnp.float32), 0.25, 1.75)
    return {"features": features, "block_loads": block_loads, "swap_counts": swap_counts, "neighbours": neighbours, "occupancy": occupancy, "conv_weights": conv_weights, "norm_gains": norm_gains}


OPPOSITE = (1, 0, 3, 2, 5, 4)

def face_slab(blocks, surface):
    number = blocks.shape[0]
    channels = blocks.shape[3] // 8
    if surface == 0:
        return blocks[:, 0]
    if surface == 1:
        return blocks[:, 7]
    if surface == 2:
        return blocks[:, :, 0]
    if surface == 3:
        return blocks[:, :, 7]
    layer_at = 0 if surface == 4 else 7
    cells = blocks.reshape(number, 8, 8, 8, channels)
    return cells[:, :, :, layer_at, :].reshape(number, 8, 8 * channels)

def block_faces(blocks):
    return jnp.stack([face_slab(blocks, surface) for surface in range(6)], axis=1)

def padded_block(blocks, halo_slabs):
    number = blocks.shape[0]
    channels = blocks.shape[3] // 8
    padded = jnp.zeros((number, 10, 10, 10 * channels), blocks.dtype)
    padded = padded.at[:, 1:9, 1:9, channels:9 * channels].set(blocks)
    padded = padded.at[:, 0, 1:9, channels:9 * channels].set(halo_slabs[:, 0])
    padded = padded.at[:, 9, 1:9, channels:9 * channels].set(halo_slabs[:, 1])
    padded = padded.at[:, 1:9, 0, channels:9 * channels].set(halo_slabs[:, 2])
    padded = padded.at[:, 1:9, 9, channels:9 * channels].set(halo_slabs[:, 3])
    padded = padded.at[:, 1:9, 1:9, 0:channels].set(halo_slabs[:, 4].reshape(number, 8, 8, channels))
    padded = padded.at[:, 1:9, 1:9, 9 * channels:].set(halo_slabs[:, 5].reshape(number, 8, 8, channels))
    return padded

def convolve_block(padded, weight):
    number = padded.shape[0]
    channels = weight.shape[1]
    volume = padded.reshape(number, 10, 10, 10, channels)
    result = jnp.zeros((number * 512, channels), jnp.float32)
    for offset in range(27):
        shift_x, shift_y, shift_z = (offset // 9, offset // 3 % 3, offset % 3)
        window = volume[:, shift_x:shift_x + 8, shift_y:shift_y + 8, shift_z:shift_z + 8, :]
        result = result + jnp.dot(window.reshape(number * 512, channels), weight[offset], preferred_element_type=jnp.float32)
    return result.reshape(number, 8, 8, 8 * channels)

def finish_layer(summed, gain_row, keep_voxel):
    number = summed.shape[0]
    channels = gain_row.shape[0]
    voxels = summed.reshape(number, 8, 8, 8, channels)
    mean_square = lax.optimization_barrier(jnp.mean(voxels * voxels, axis=-1, keepdims=True))
    scaled = voxels * lax.rsqrt(mean_square + 1e-05) * gain_row
    output = jnp.where(keep_voxel, jnp.maximum(scaled, 0.0), 0.0)
    return output.astype(jnp.bfloat16).reshape(number, 8, 8, 8 * channels)

def rebalance(blocks, filled, swap_counts):
    groups, owners = filled.shape
    owner_ids = jnp.arange(owners)
    places = jnp.arange(CAP)[None, None, :]
    group_base = (jnp.arange(groups) * owners)[:, None, None]
    is_left = owner_ids % 2 == 0
    leader = owner_ids - owner_ids % 2
    partner = jnp.clip(jnp.where(is_left, owner_ids + 1, owner_ids - 1), 0, owners - 1)
    swap_size = swap_counts[:, 0, :][:, leader][:, :, None]
    giving = jnp.maximum(swap_size, 0)
    taking = jnp.maximum(-swap_size, 0)
    own_fill = filled[:, :, None]
    other_fill = filled[:, partner][:, :, None]
    left_own = places < own_fill - giving
    left_valid = left_own | (places >= own_fill) & (places < own_fill + taking)
    left_slot = jnp.where(left_own, places, places - own_fill)
    right_other = places < giving
    right_valid = places < giving + own_fill - taking
    right_slot = jnp.where(right_other, other_fill - giving + places, places - giving + taking)
    side_left = is_left[None, :, None]
    from_self = jnp.where(side_left, left_own, jnp.logical_not(right_other))
    is_valid = jnp.where(side_left, left_valid, right_valid)
    slot_index = jnp.where(side_left, left_slot, right_slot)
    source_owner = jnp.where(from_self, owner_ids[None, :, None], partner[None, :, None])
    gather_at = (group_base + source_owner) * CAP + slot_index
    gather_at = jnp.clip(jnp.where(is_valid, gather_at, 0), 0, blocks.shape[0] - 1).astype(jnp.int32)
    carried = jnp.take(blocks, gather_at.reshape(-1), axis=0)
    blocks = jnp.where(is_valid.reshape(-1)[:, None, None, None], carried, jnp.zeros_like(carried))
    filled = jnp.where(is_left[None, :], filled - swap_size[:, :, 0], filled + swap_size[:, :, 0])
    flows = swap_counts[:, 1, :]
    nothing = jnp.zeros((groups, 1), flows.dtype)
    right_flow = jnp.concatenate([flows[:, :owners - 1], nothing], axis=1)
    left_flow = jnp.concatenate([nothing, flows[:, :owners - 1]], axis=1)
    from_left = jnp.maximum(left_flow, 0)[:, :, None]
    to_left = jnp.maximum(-left_flow, 0)[:, :, None]
    to_right = jnp.maximum(right_flow, 0)[:, :, None]
    from_right = jnp.maximum(-right_flow, 0)[:, :, None]
    own_fill = filled[:, :, None]
    below_fill = jnp.concatenate([nothing, filled[:, :owners - 1]], axis=1)[:, :, None]
    middle = own_fill - to_left - to_right
    is_below = places < from_left
    is_self = jnp.logical_not(is_below) & (places < from_left + middle)
    is_above = (places >= from_left + middle) & (places < from_left + middle + from_right)
    owner_col = owner_ids[None, :, None]
    source_owner = jnp.where(is_below, owner_col - 1, jnp.where(is_above, owner_col + 1, owner_col))
    source_owner = jnp.clip(source_owner, 0, owners - 1)
    slot_index = jnp.where(is_below, below_fill - from_left + places, jnp.where(is_self, places - from_left + to_left, places - from_left - middle))
    is_valid = is_below | is_self | is_above
    gather_at = (group_base + source_owner) * CAP + slot_index
    gather_at = jnp.clip(jnp.where(is_valid, gather_at, 0), 0, blocks.shape[0] - 1).astype(jnp.int32)
    carried = jnp.take(blocks, gather_at.reshape(-1), axis=0)
    blocks = jnp.where(is_valid.reshape(-1)[:, None, None, None], carried, jnp.zeros_like(carried))
    filled = filled + left_flow - right_flow
    return (blocks, filled)

def gather_halos(values, neighbours, owners):
    total_slots = values.shape[0]
    surfaces = block_faces(values)
    source = jnp.where(neighbours >= 0, neighbours // CAP, 0)
    within = neighbours % CAP
    device_of = (jnp.arange(total_slots) // CAP)[:, None]
    group_of = device_of // owners
    position = device_of % owners
    step_group = jnp.array([0, 0, 0, -1, 1])[source]
    step_owner = jnp.array([0, -1, 1, 0, 0])[source]
    anchor = ((group_of + step_group) * owners + position + step_owner) * CAP + within
    opposite = jnp.array(OPPOSITE)[None, :]
    lookup = jnp.clip(anchor * 6 + opposite, 0, total_slots * 6 - 1).astype(jnp.int32)
    picked = jnp.take(surfaces.reshape(total_slots * 6, 8, surfaces.shape[3]), lookup.reshape(-1), axis=0)
    picked = picked.reshape(total_slots, 6, 8, surfaces.shape[3])
    return jnp.where((neighbours >= 0)[:, :, None, None], picked, jnp.zeros_like(picked))

def reference(features, block_loads, swap_counts, neighbours, occupancy, conv_weights, norm_gains):
    groups, owners = (N_GRP, N_CURVE)
    devices = groups * owners
    channels = CH
    blocks, filled = rebalance(features, block_loads.reshape(groups, owners), swap_counts)
    is_live = jnp.arange(CAP)[None, :] < filled.reshape(-1, 1)
    keep_voxel = (is_live.reshape(-1, 1) & (occupancy > 0)).reshape(-1, 8, 8, 8, 1)
    values = jnp.where(keep_voxel, blocks.reshape(-1, 8, 8, 8, channels), 0.0)
    values = values.astype(jnp.bfloat16).reshape(blocks.shape)
    for layer_no in range(LAYERS):
        halo_slabs = gather_halos(values, neighbours, owners)

        def one_device(pieces):
            own_blocks, slabs_here, kept_voxel = pieces
            padded = padded_block(own_blocks, slabs_here)
            summed = convolve_block(padded, conv_weights[layer_no])
            return finish_layer(summed, norm_gains[layer_no], kept_voxel)
        values = lax.map(one_device, (values.reshape(devices, CAP, 8, 8, 8 * channels), halo_slabs.reshape(devices, CAP, 6, 8, 8 * channels), keep_voxel.reshape(devices, CAP, 8, 8, 8, 1)))
        values = values.reshape(blocks.shape)
    return values
```

```python
import functools

import jax
import jax.numpy as jnp
from jax import lax
from jax.experimental import pallas as pl
from jax.experimental.pallas import tpu as pltpu
from jax.sharding import PartitionSpec as P

F32 = jnp.float32
BF16 = jnp.bfloat16
I32 = jnp.int32
MESH = pl.DeviceIdType.MESH


def lanes_low():
    return lax.broadcasted_iota(I32, (8, 128), 1) < 64


def half_turn(tile):
    return pltpu.roll(tile, 64, 1)


def widen(tiles, low_side, high_side):
    low = lanes_low()
    turned = [half_turn(t) for t in tiles]
    out = [jnp.where(low, low_side, turned[0])]
    for t in range(1, 4):
        out.append(jnp.where(low, turned[t - 1], turned[t]))
    out.append(jnp.where(low, turned[3], high_side))
    return jnp.concatenate(out, axis=1)


def kernel(
    groups,
    owners,
    feat,
    loads,
    swaps,
    nbrs,
    occ,
    wts,
    gains,
    out,
    blocks,
    moved,
    outgoing,
    loads_s,
    swaps_s,
    nbrs_s,
    asked_s,
    own_at,
    far_at,
    kind_at,
    occ_v,
    w_v,
    g_v,
    banded,
    mask,
    nat,
    faces,
    send_f,
    recv_first,
    recv_second,
    lhs,
    y_rows,
    in_sems,
    list_send,
    list_recv,
    block_send,
    block_recv,
    face_send,
    face_recv,
):
    grp = lax.axis_index("grp")
    own = lax.axis_index("curve")
    odd = lax.rem(own, 2) == 1
    before = (grp, lax.rem(own + owners - 1, owners))
    after = (grp, lax.rem(own + 1, owners))
    below = (lax.rem(grp + groups - 1, groups), own)
    above = (lax.rem(grp + 1, groups), own)
    sides = (before, after, below, above)

    local = [
        pltpu.make_async_copy(feat, blocks, in_sems.at[0]),
        pltpu.make_async_copy(loads, loads_s, in_sems.at[1]),
        pltpu.make_async_copy(swaps, swaps_s, in_sems.at[2]),
        pltpu.make_async_copy(nbrs, nbrs_s, in_sems.at[3]),
        pltpu.make_async_copy(occ, occ_v, in_sems.at[4]),
        pltpu.make_async_copy(wts, w_v, in_sems.at[5]),
        pltpu.make_async_copy(gains, g_v, in_sems.at[6]),
    ]
    for copy in local:
        copy.start()

    barrier = pltpu.get_barrier_semaphore()
    for device in sides:
        pl.semaphore_signal(barrier, inc=1, device_id=device, device_id_type=MESH)
    pl.semaphore_wait(barrier, 4)

    lists = [
        pltpu.make_async_remote_copy(
            src_ref=nbrs,
            dst_ref=asked_s.at[i ^ 1],
            send_sem=list_send.at[i],
            recv_sem=list_recv.at[i ^ 1],
            device_id=sides[i],
            device_id_type=MESH,
        )
        for i in range(4)
    ]
    for copy in lists:
        copy.start()

    local[1].wait()
    local[0].wait()
    load = loads_s[0]
    tail = jnp.maximum(load - 1, 0)
    outgoing[2] = blocks[jnp.where(odd, tail, 0)]
    partner = (grp, own + 1 - 2 * lax.rem(own, 2))
    across = (grp, lax.rem(own + owners - 1 + 2 * lax.rem(own, 2), owners))
    cross_copy = pltpu.make_async_remote_copy(
        src_ref=outgoing.at[pl.ds(2, 1)],
        dst_ref=moved.at[pl.ds(2, 1)],
        send_sem=block_send.at[0],
        recv_sem=block_recv.at[0],
        device_id=across,
        device_id_type=MESH,
    )
    cross_copy.start()
    outgoing[0] = blocks[jnp.where(odd, 0, jnp.maximum(load - 2, 0))]
    outgoing[1] = blocks[jnp.where(odd, 1, tail)]
    pair_copy = pltpu.make_async_remote_copy(
        src_ref=outgoing.at[pl.ds(0, 2)],
        dst_ref=moved.at[pl.ds(0, 2)],
        send_sem=block_send.at[1],
        recv_sem=block_recv.at[1],
        device_id=partner,
        device_id_type=MESH,
    )
    pair_copy.start()

    for copy in local[2:]:
        copy.wait()

    zero_w = jnp.zeros((64, 64), BF16)
    for layer in range(2):
        for dx in range(3):
            for dy in range(3):
                w = [w_v[layer, dx * 9 + dy * 3 + dz] for dz in range(3)]
                rows = [(w[0], zero_w), (w[1], w[0]), (w[2], w[1]), (zero_w, w[2])]
                for zi in range(4):
                    banded[layer, pl.ds((dy * 4 + zi) * 64, 64), pl.ds(dx * 128, 128)] = (
                        jnp.concatenate(rows[zi], axis=1)
                    )

    swap = swaps_s[0, 0, own - lax.rem(own, 2)]
    flow_in = jnp.where(own > 0, swaps_s[0, 1, jnp.maximum(own - 1, 0)], 0)
    flow_out = jnp.where(own < owners - 1, swaps_s[0, 1, own], 0)
    first_load = load + jnp.where(odd, swap, -swap)
    came = jnp.maximum(flow_in, 0)
    dropped = jnp.maximum(-flow_in, 0)
    middle = first_load - dropped - jnp.maximum(flow_out, 0)
    taken = jnp.maximum(-flow_out, 0)
    final = first_load + flow_in - flow_out
    came_at = jnp.where(odd, jnp.where(swap > 0, 4, jnp.where(swap < 0, 0, 5)), 6)
    taken_at = jnp.where(odd, 6, jnp.where(swap > 0, tail, jnp.where(swap < 0, 5, 4)))
    places = []
    for j in range(4):
        i = j - came + dropped
        even_at = jnp.where(i < load - jnp.maximum(swap, 0), i, 4)
        odd_at = jnp.where((swap > 0) & (i == 0), 5, i - swap)
        kept_at = jnp.where(odd, odd_at, even_at)
        at = jnp.where(
            j < came,
            came_at,
            jnp.where(j < came + middle, kept_at, jnp.where(j < came + middle + taken, taken_at, 0)),
        )
        places.append(jnp.clip(at, 0, 6))

    block_no = lax.broadcasted_iota(I32, (4, 512), 0)
    occupied = jnp.where((block_no < final) & (occ_v[...] > 0), 1.0, 0.0).astype(F32)
    lane3 = lax.broadcasted_iota(I32, (4, 8, 128), 2)
    sub3 = lax.broadcasted_iota(I32, (4, 8, 128), 1)
    strips = []
    for x in range(8):
        strip = occupied[:, 128 * (x // 2) : 128 * (x // 2) + 128]
        wide = jnp.broadcast_to(strip[:, None, :], (4, 8, 128))
        pick = (lane3 // 8) == (sub3 + 8 * (x % 2))
        strips.append(jnp.where(pick, wide, 0.0).reshape(32, 128))
    strips = jnp.concatenate(strips, axis=0).astype(BF16)
    spread = jnp.where(
        lax.rem(lax.broadcasted_iota(I32, (128, 512), 0), 8)
        == lax.broadcasted_iota(I32, (128, 512), 1) // 64,
        1.0,
        0.0,
    ).astype(BF16)
    mask[...] = jnp.dot(strips, spread, preferred_element_type=F32)

    def rank_step(b, counts):
        counts = list(counts)
        for f in range(6):
            v = nbrs_s[b, f]
            s = lax.shift_right_arithmetic(v, 2)
            rank = jnp.int32(0)
            for i in range(4):
                hit = s == i + 1
                rank = jnp.where(hit, 4 * i + counts[i], rank)
                counts[i] = counts[i] + hit.astype(I32)
            kind_at[b, f] = s
            own_at[b, f] = jnp.where(v >= 0, (v & 3) * 6 + (f ^ 1), 0)
            far_at[b, f] = jnp.clip(rank, 0, 15)
        return tuple(counts)

    lax.fori_loop(0, 4, rank_step, (jnp.int32(0),) * 4)

    for copy in lists:
        copy.wait_recv()

    def ask_step(b, state):
        state = [list(row) for row in state]
        for f in range(6):
            for i in range(4):
                v = asked_s[i, b, f]
                count = state[i][4]
                hit = lax.shift_right_arithmetic(v, 2) == (i ^ 1) + 1
                face = (v & 3) * 6 + (f ^ 1)
                for j in range(4):
                    state[i][j] = jnp.where(hit & (count == j), face, state[i][j])
                state[i][4] = count + hit.astype(I32)
        return tuple(tuple(row) for row in state)

    asked = lax.fori_loop(0, 4, ask_step, ((jnp.int32(0),) * 5,) * 4)

    cross_copy.wait_recv()
    pair_copy.wait_recv()
    for j in range(4):
        mine = blocks[jnp.minimum(places[j], 3)].astype(F32)
        other = moved[jnp.maximum(places[j] - 4, 0)].astype(F32)
        block = jnp.where(places[j] < 4, mine, other)
        for x in range(8):
            rows = pl.ds(x * 32 + j * 8, 8)
            kept = jnp.where(mask[rows, :] > 0.5, block[8 * x : 8 * x + 8], 0.0)
            for t in range(4):
                nat[t, rows, :] = kept[:, 128 * t : 128 * t + 128]

    low = lanes_low()
    sub = lax.broadcasted_iota(I32, (8, 640), 0)
    none8 = jnp.zeros((8, 128), F32)
    group_lane = lax.broadcasted_iota(I32, (256, 128), 1) // 64
    group_row = lax.rem(lax.broadcasted_iota(I32, (256, 128), 0), 128) // 64
    averager = jnp.where(group_lane == group_row, 1.0 / 64.0, 0.0).astype(BF16)

    for layer in range(2):
        recv_f = (recv_first, recv_second)[layer]
        for b in range(4):
            for f in range(2):
                r = 7 * f * 32 + b * 8
                face = [nat[t, pl.ds(r, 8), :] for t in range(4)]
                faces[b * 6 + f] = jnp.concatenate(face, axis=0).astype(BF16)
                face = [
                    nat[t, pl.ds(b * 8 + 7 * f, 8, stride=32), :] for t in range(4)
                ]
                faces[b * 6 + 2 + f] = jnp.concatenate(face, axis=0).astype(BF16)
            face = []
            for x in range(4):
                here = nat[0, pl.ds(x * 32 + b * 8, 8), :]
                there = nat[0, pl.ds((x + 4) * 32 + b * 8, 8), :]
                face.append(jnp.where(low, here, half_turn(there)))
            faces[b * 6 + 4] = jnp.concatenate(face, axis=0).astype(BF16)
            face = []
            for x in range(4):
                here = nat[3, pl.ds(x * 32 + b * 8, 8), :]
                there = nat[3, pl.ds((x + 4) * 32 + b * 8, 8), :]
                face.append(jnp.where(low, half_turn(here), there))
            faces[b * 6 + 5] = jnp.concatenate(face, axis=0).astype(BF16)
        copies = []
        for i in range(4):
            for j in range(4):
                send_f[layer, 4 * i + j] = faces[asked[i][j]]
            copy = pltpu.make_async_remote_copy(
                src_ref=send_f.at[layer, pl.ds(4 * i, 4)],
                dst_ref=recv_f.at[pl.ds(4 * (i ^ 1), 4)],
                send_sem=face_send.at[layer, i],
                recv_sem=face_recv.at[layer, i ^ 1],
                device_id=sides[i],
                device_id_type=MESH,
            )
            copy.start()
            copies.append(copy)
        for copy in copies:
            copy.wait()

        def halo(b, f):
            kind = kind_at[b, f]
            mine = faces[own_at[b, f]].astype(F32)
            far = recv_f[far_at[b, f]].astype(F32)
            zero = jnp.zeros((32, 128), F32)
            both = jnp.where(kind == 0, mine, jnp.where(kind > 0, far, zero))
            return [both[8 * t : 8 * t + 8] for t in range(4)]

        halos = [[halo(b, f) for f in range(6)] for b in range(4)]
        for b in range(4):
            for f in range(2):
                y_rows[f, b] = widen(halos[b][2 + f], none8, none8)
        for p in range(10):
            for pair in range(2):
                parts = [[], [], []]
                for b in (2 * pair, 2 * pair + 1):
                    if p == 0 or p == 9:
                        centre = widen(halos[b][0 if p == 0 else 1], none8, none8)
                        first = jnp.zeros((8, 640), F32)
                        last = first
                    else:
                        x = p - 1
                        tiles = [
                            nat[t, pl.ds(x * 32 + b * 8, 8), :] for t in range(4)
                        ]
                        z_low = halos[b][4][x % 4]
                        z_high = halos[b][5][x % 4]
                        if x >= 4:
                            z_low = half_turn(z_low)
                        else:
                            z_high = half_turn(z_high)
                        centre = widen(tiles, z_low, z_high)
                        first = jnp.broadcast_to(y_rows[0, b, pl.ds(x, 1), :], (8, 640))
                        last = jnp.broadcast_to(y_rows[1, b, pl.ds(x, 1), :], (8, 640))
                    parts[0].append(jnp.where(sub == 0, first, pltpu.roll(centre, 1, 0)))
                    parts[1].append(centre)
                    parts[2].append(jnp.where(sub == 7, last, pltpu.roll(centre, 7, 0)))
                for dy in range(3):
                    lhs[dy, pl.ds(p * 32 + pair * 16, 16), :] = jnp.concatenate(
                        parts[dy], axis=0
                    ).astype(BF16)

        gain = g_v[pl.ds(layer, 1), :]
        gain = jnp.concatenate([gain, gain], axis=1)
        for k in range(4):
            window = jnp.concatenate(
                [lhs[dy, :, pl.ds(128 * k, 256)] for dy in range(3)], axis=1
            )
            r = jnp.dot(window, banded[layer], preferred_element_type=F32)
            total = r[0:256, 0:128] + r[32:288, 128:256] + r[64:320, 256:384]
            square = total * total
            coarse = square.astype(BF16)
            fine = (square - coarse.astype(F32)).astype(BF16)
            mean = jnp.dot(
                jnp.concatenate([coarse, fine], axis=1), averager, preferred_element_type=F32
            )
            scaled = total * lax.rsqrt(mean + 1e-5) * gain
            keep = mask[:, pl.ds(128 * k, 128)] > 0.5
            done = jnp.where(keep, jnp.maximum(scaled, 0.0), 0.0)
            if layer == 0:
                nat[k] = done
            else:
                cells = done.reshape(8, 4, 8, 128)
                for b in range(4):
                    out[b, :, :, pl.ds(128 * k, 128)] = cells[:, b].astype(BF16)

    for copy in lists:
        copy.wait_send()
    cross_copy.wait_send()
    pair_copy.wait_send()


def local_program(groups, owners, features, block_loads, swap_counts, neighbours, occupancy, conv_weights, norm_gains):
    any_space = pl.BlockSpec(memory_space=pl.ANY)
    return pl.pallas_call(
        functools.partial(kernel, groups, owners),
        out_shape=jax.ShapeDtypeStruct((4, 8, 8, 512), BF16),
        in_specs=[any_space] * 7,
        out_specs=pl.BlockSpec(memory_space=pltpu.VMEM),
        scratch_shapes=[
            pltpu.VMEM((4, 64, 512), BF16),
            pltpu.VMEM((3, 64, 512), BF16),
            pltpu.VMEM((3, 64, 512), BF16),
            pltpu.SMEM((1,), I32),
            pltpu.SMEM((1, 2, owners), I32),
            pltpu.SMEM((4, 6), I32),
            pltpu.SMEM((4, 4, 6), I32),
            pltpu.SMEM((4, 6), I32),
            pltpu.SMEM((4, 6), I32),
            pltpu.SMEM((4, 6), I32),
            pltpu.VMEM((4, 512), I32),
            pltpu.VMEM((2, 27, 64, 64), BF16),
            pltpu.VMEM((2, 64), F32),
            pltpu.VMEM((2, 768, 384), BF16),
            pltpu.VMEM((256, 512), F32),
            pltpu.VMEM((4, 256, 128), F32),
            pltpu.VMEM((24, 32, 128), BF16),
            pltpu.VMEM((2, 16, 32, 128), BF16),
            pltpu.VMEM((16, 32, 128), BF16),
            pltpu.VMEM((16, 32, 128), BF16),
            pltpu.VMEM((3, 320, 640), BF16),
            pltpu.VMEM((2, 4, 8, 640), F32),
            pltpu.SemaphoreType.DMA((7,)),
            pltpu.SemaphoreType.DMA((4,)),
            pltpu.SemaphoreType.DMA((4,)),
            pltpu.SemaphoreType.DMA((2,)),
            pltpu.SemaphoreType.DMA((2,)),
            pltpu.SemaphoreType.DMA((2, 4)),
            pltpu.SemaphoreType.DMA((2, 4)),
        ],
        compiler_params=pltpu.CompilerParams(
            collective_id=0, has_side_effects=True, vmem_limit_bytes=40 * 1024 * 1024
        ),
    )(features.reshape(4, 64, 512), block_loads, swap_counts, neighbours, occupancy, conv_weights, norm_gains)


def solution(mesh):
    groups, owners = mesh.shape["grp"], mesh.shape["curve"]
    return jax.shard_map(
        functools.partial(local_program, groups, owners),
        mesh=mesh,
        in_specs=(
            P(("grp", "curve"), None, None, None),
            P(("grp", "curve")),
            P("grp", None, None),
            P(("grp", "curve"), None),
            P(("grp", "curve"), None),
            P(),
            P(),
        ),
        out_specs=P(("grp", "curve"), None, None, None),
        check_vma=False,
    )
```

```python
import functools
import types

import jax
import jax.numpy as jnp
from jax import lax
from jax.experimental import pallas as pl
from jax.experimental.pallas import tpu as pltpu
from jax.sharding import PartitionSpec as P

F32 = jnp.float32
BF16 = jnp.bfloat16
I32 = jnp.int32
MESH = pl.DeviceIdType.MESH

SCRATCH = dict(
    blocks=pltpu.VMEM((4, 64, 512), BF16),
    moved=pltpu.VMEM((3, 64, 512), BF16),
    outgoing=pltpu.VMEM((3, 64, 512), BF16),
    loads_s=pltpu.SMEM((1,), I32),
    swaps_s=pltpu.SMEM((1, 2, 32), I32),
    nbrs_s=pltpu.SMEM((4, 6), I32),
    asked_s=pltpu.SMEM((4, 4, 6), I32),
    own_at=pltpu.SMEM((4, 6), I32),
    far_at=pltpu.SMEM((4, 6), I32),
    kind_at=pltpu.SMEM((4, 6), I32),
    occ_v=pltpu.VMEM((4, 512), I32),
    w_v=pltpu.VMEM((2, 27, 64, 64), BF16),
    g_v=pltpu.VMEM((2, 64), F32),
    banded=pltpu.VMEM((2, 768, 384), BF16),
    mask=pltpu.VMEM((256, 512), F32),
    nat=pltpu.VMEM((4, 256, 128), F32),
    faces=pltpu.VMEM((24, 32, 128), BF16),
    send_f=pltpu.VMEM((2, 16, 32, 128), BF16),
    recv_first=pltpu.VMEM((16, 32, 128), BF16),
    recv_second=pltpu.VMEM((16, 32, 128), BF16),
    lhs=pltpu.VMEM((3, 320, 640), BF16),
    y_rows=pltpu.VMEM((2, 4, 8, 640), F32),
    in_sems=pltpu.SemaphoreType.DMA((7,)),
    list_send=pltpu.SemaphoreType.DMA((4,)),
    list_recv=pltpu.SemaphoreType.DMA((4,)),
    block_send=pltpu.SemaphoreType.DMA((2,)),
    block_recv=pltpu.SemaphoreType.DMA((2,)),
    face_send=pltpu.SemaphoreType.DMA((2, 4)),
    face_recv=pltpu.SemaphoreType.DMA((2, 4)),
)
OPERANDS = ("feat", "loads", "swaps", "nbrs", "occ", "wts", "gains", "out")


def lanes_low():
    return lax.broadcasted_iota(I32, (8, 128), 1) < 64


def half_turn(tile):
    return pltpu.roll(tile, 64, 1)


def widen(tiles, low_side, high_side):
    low = lanes_low()
    turned = [half_turn(t) for t in tiles]
    out = [jnp.where(low, low_side, turned[0])]
    for t in range(1, 4):
        out.append(jnp.where(low, turned[t - 1], turned[t]))
    out.append(jnp.where(low, turned[3], high_side))
    return jnp.concatenate(out, axis=1)


def build_weights(r):
    zero_w = jnp.zeros((64, 64), BF16)
    for layer in range(2):
        for dx in range(3):
            for dy in range(3):
                w = [r.w_v[layer, dx * 9 + dy * 3 + dz] for dz in range(3)]
                rows = [(w[0], zero_w), (w[1], w[0]), (w[2], w[1]), (zero_w, w[2])]
                for zi in range(4):
                    r.banded[layer, pl.ds((dy * 4 + zi) * 64, 64), pl.ds(dx * 128, 128)] = (
                        jnp.concatenate(rows[zi], axis=1)
                    )


def settle_places(r, owners, own, odd, load, tail):
    swap = r.swaps_s[0, 0, own - lax.rem(own, 2)]
    flow_in = jnp.where(own > 0, r.swaps_s[0, 1, jnp.maximum(own - 1, 0)], 0)
    flow_out = jnp.where(own < owners - 1, r.swaps_s[0, 1, own], 0)
    first_load = load + jnp.where(odd, swap, -swap)
    came = jnp.maximum(flow_in, 0)
    dropped = jnp.maximum(-flow_in, 0)
    middle = first_load - dropped - jnp.maximum(flow_out, 0)
    taken = jnp.maximum(-flow_out, 0)
    final = first_load + flow_in - flow_out
    came_at = jnp.where(odd, jnp.where(swap > 0, 4, jnp.where(swap < 0, 0, 5)), 6)
    taken_at = jnp.where(odd, 6, jnp.where(swap > 0, tail, jnp.where(swap < 0, 5, 4)))
    places = []
    for j in range(4):
        i = j - came + dropped
        even_at = jnp.where(i < load - jnp.maximum(swap, 0), i, 4)
        odd_at = jnp.where((swap > 0) & (i == 0), 5, i - swap)
        kept_at = jnp.where(odd, odd_at, even_at)
        at = jnp.where(
            j < came,
            came_at,
            jnp.where(j < came + middle, kept_at, jnp.where(j < came + middle + taken, taken_at, 0)),
        )
        places.append(jnp.clip(at, 0, 6))
    return places, final


def build_mask(r, final):
    block_no = lax.broadcasted_iota(I32, (4, 512), 0)
    occupied = jnp.where((block_no < final) & (r.occ_v[...] > 0), 1.0, 0.0).astype(F32)
    lane3 = lax.broadcasted_iota(I32, (4, 8, 128), 2)
    sub3 = lax.broadcasted_iota(I32, (4, 8, 128), 1)
    strips = []
    for x in range(8):
        strip = occupied[:, 128 * (x // 2) : 128 * (x // 2) + 128]
        wide = jnp.broadcast_to(strip[:, None, :], (4, 8, 128))
        pick = (lane3 // 8) == (sub3 + 8 * (x % 2))
        strips.append(jnp.where(pick, wide, 0.0).reshape(32, 128))
    strips = jnp.concatenate(strips, axis=0).astype(BF16)
    spread = jnp.where(
        lax.rem(lax.broadcasted_iota(I32, (128, 512), 0), 8)
        == lax.broadcasted_iota(I32, (128, 512), 1) // 64,
        1.0,
        0.0,
    ).astype(BF16)
    r.mask[...] = jnp.dot(strips, spread, preferred_element_type=F32)


def rank_halos(r):
    def rank_step(b, counts):
        counts = list(counts)
        for f in range(6):
            v = r.nbrs_s[b, f]
            s = lax.shift_right_arithmetic(v, 2)
            rank = jnp.int32(0)
            for i in range(4):
                hit = s == i + 1
                rank = jnp.where(hit, 4 * i + counts[i], rank)
                counts[i] = counts[i] + hit.astype(I32)
            r.kind_at[b, f] = s
            r.own_at[b, f] = jnp.where(v >= 0, (v & 3) * 6 + (f ^ 1), 0)
            r.far_at[b, f] = jnp.clip(rank, 0, 15)
        return tuple(counts)

    lax.fori_loop(0, 4, rank_step, (jnp.int32(0),) * 4)


def rank_asked(r):
    def ask_step(b, state):
        state = [list(row) for row in state]
        for f in range(6):
            for i in range(4):
                v = r.asked_s[i, b, f]
                count = state[i][4]
                hit = lax.shift_right_arithmetic(v, 2) == (i ^ 1) + 1
                face = (v & 3) * 6 + (f ^ 1)
                for j in range(4):
                    state[i][j] = jnp.where(hit & (count == j), face, state[i][j])
                state[i][4] = count + hit.astype(I32)
        return tuple(tuple(row) for row in state)

    return lax.fori_loop(0, 4, ask_step, ((jnp.int32(0),) * 5,) * 4)


def settle(r, places):
    for j in range(4):
        mine = r.blocks[jnp.minimum(places[j], 3)].astype(F32)
        other = r.moved[jnp.maximum(places[j] - 4, 0)].astype(F32)
        block = jnp.where(places[j] < 4, mine, other)
        for x in range(8):
            rows = pl.ds(x * 32 + j * 8, 8)
            kept = jnp.where(r.mask[rows, :] > 0.5, block[8 * x : 8 * x + 8], 0.0)
            for t in range(4):
                r.nat[t, rows, :] = kept[:, 128 * t : 128 * t + 128]


def build_faces(r):
    low = lanes_low()
    for b in range(4):
        for f in range(2):
            face = [r.nat[t, pl.ds(7 * f * 32 + b * 8, 8), :] for t in range(4)]
            r.faces[b * 6 + f] = jnp.concatenate(face, axis=0).astype(BF16)
            face = [r.nat[t, pl.ds(b * 8 + 7 * f, 8, stride=32), :] for t in range(4)]
            r.faces[b * 6 + 2 + f] = jnp.concatenate(face, axis=0).astype(BF16)
        for f in range(2):
            face = []
            for x in range(4):
                here = r.nat[3 * f, pl.ds(x * 32 + b * 8, 8), :]
                there = r.nat[3 * f, pl.ds((x + 4) * 32 + b * 8, 8), :]
                if f == 0:
                    there = half_turn(there)
                else:
                    here = half_turn(here)
                face.append(jnp.where(low, here, there))
            r.faces[b * 6 + 4 + f] = jnp.concatenate(face, axis=0).astype(BF16)


def pick_faces(r, layer, asked):
    for i in range(4):
        for j in range(4):
            r.send_f[layer, 4 * i + j] = r.faces[asked[i][j]]


def read_halos(r, recv_f):
    def halo(b, f):
        kind = r.kind_at[b, f]
        mine = r.faces[r.own_at[b, f]].astype(F32)
        far = recv_f[r.far_at[b, f]].astype(F32)
        zero = jnp.zeros((32, 128), F32)
        both = jnp.where(kind == 0, mine, jnp.where(kind > 0, far, zero))
        return [both[8 * t : 8 * t + 8] for t in range(4)]

    return [[halo(b, f) for f in range(6)] for b in range(4)]


def build_lhs(r, halos):
    sub = lax.broadcasted_iota(I32, (8, 640), 0)
    none8 = jnp.zeros((8, 128), F32)
    for b in range(4):
        for f in range(2):
            r.y_rows[f, b] = widen(halos[b][2 + f], none8, none8)
    for p in range(10):
        for pair in range(2):
            parts = [[], [], []]
            for b in (2 * pair, 2 * pair + 1):
                if p == 0 or p == 9:
                    centre = widen(halos[b][0 if p == 0 else 1], none8, none8)
                    first = jnp.zeros((8, 640), F32)
                    last = first
                else:
                    x = p - 1
                    tiles = [r.nat[t, pl.ds(x * 32 + b * 8, 8), :] for t in range(4)]
                    z_low = halos[b][4][x % 4]
                    z_high = halos[b][5][x % 4]
                    if x >= 4:
                        z_low = half_turn(z_low)
                    else:
                        z_high = half_turn(z_high)
                    centre = widen(tiles, z_low, z_high)
                    first = jnp.broadcast_to(r.y_rows[0, b, pl.ds(x, 1), :], (8, 640))
                    last = jnp.broadcast_to(r.y_rows[1, b, pl.ds(x, 1), :], (8, 640))
                parts[0].append(jnp.where(sub == 0, first, pltpu.roll(centre, 1, 0)))
                parts[1].append(centre)
                parts[2].append(jnp.where(sub == 7, last, pltpu.roll(centre, 7, 0)))
            for dy in range(3):
                r.lhs[dy, pl.ds(p * 32 + pair * 16, 16), :] = jnp.concatenate(
                    parts[dy], axis=0
                ).astype(BF16)


def convolve(r, layer):
    group_lane = lax.broadcasted_iota(I32, (256, 128), 1) // 64
    group_row = lax.rem(lax.broadcasted_iota(I32, (256, 128), 0), 128) // 64
    averager = jnp.where(group_lane == group_row, 1.0 / 64.0, 0.0).astype(BF16)
    gain = r.g_v[pl.ds(layer, 1), :]
    gain = jnp.concatenate([gain, gain], axis=1)
    for k in range(4):
        window = jnp.concatenate([r.lhs[dy, :, pl.ds(128 * k, 256)] for dy in range(3)], axis=1)
        three = jnp.dot(window, r.banded[layer], preferred_element_type=F32)
        total = three[0:256, 0:128] + three[32:288, 128:256] + three[64:320, 256:384]
        square = total * total
        coarse = square.astype(BF16)
        fine = (square - coarse.astype(F32)).astype(BF16)
        mean = jnp.dot(
            jnp.concatenate([coarse, fine], axis=1), averager, preferred_element_type=F32
        )
        scaled = total * lax.rsqrt(mean + 1e-5) * gain
        keep = r.mask[:, pl.ds(128 * k, 128)] > 0.5
        done = jnp.where(keep, jnp.maximum(scaled, 0.0), 0.0)
        if layer == 0:
            r.nat[k] = done
        else:
            cells = done.reshape(8, 4, 8, 128)
            for b in range(4):
                r.out[b, :, :, pl.ds(128 * k, 128)] = cells[:, b].astype(BF16)


def kernel(groups, owners, *refs):
    r = types.SimpleNamespace(**dict(zip(OPERANDS + tuple(SCRATCH), refs)))
    grp = lax.axis_index("grp")
    own = lax.axis_index("curve")
    odd = lax.rem(own, 2) == 1
    sides = (
        (grp, jnp.maximum(own - 1, 0)),
        (grp, jnp.minimum(own + 1, owners - 1)),
        (jnp.maximum(grp - 1, 0), own),
        (jnp.minimum(grp + 1, groups - 1), own),
    )
    there = (own > 0, own < owners - 1, grp > 0, grp < groups - 1)

    def for_sides(step):
        for i in range(4):
            pl.when(there[i])(functools.partial(step, i))

    local = [
        pltpu.make_async_copy(source, target, r.in_sems.at[i])
        for i, (source, target) in enumerate(
            (
                (r.feat, r.blocks),
                (r.loads, r.loads_s),
                (r.swaps, r.swaps_s),
                (r.nbrs, r.nbrs_s),
                (r.occ, r.occ_v),
                (r.wts, r.w_v),
                (r.gains, r.g_v),
            )
        )
    ]
    for copy in local:
        copy.start()

    barrier = pltpu.get_barrier_semaphore()
    for_sides(
        lambda i: pl.semaphore_signal(barrier, inc=1, device_id=sides[i], device_id_type=MESH)
    )
    pl.semaphore_wait(barrier, sum(flag.astype(I32) for flag in there))

    lists = [
        pltpu.make_async_remote_copy(
            src_ref=r.nbrs,
            dst_ref=r.asked_s.at[i ^ 1],
            send_sem=r.list_send.at[i],
            recv_sem=r.list_recv.at[i ^ 1],
            device_id=sides[i],
            device_id_type=MESH,
        )
        for i in range(4)
    ]
    for_sides(lambda i: lists[i].start())

    local[1].wait()
    local[0].wait()
    load = r.loads_s[0]
    tail = jnp.maximum(load - 1, 0)
    r.outgoing[2] = r.blocks[jnp.where(odd, tail, 0)]
    partner = (grp, own + 1 - 2 * lax.rem(own, 2))
    across = (grp, jnp.clip(own - 1 + 2 * lax.rem(own, 2), 0, owners - 1))
    has_across = (own > 0) & (own < owners - 1)
    cross_copy = pltpu.make_async_remote_copy(
        src_ref=r.outgoing.at[pl.ds(2, 1)],
        dst_ref=r.moved.at[pl.ds(2, 1)],
        send_sem=r.block_send.at[0],
        recv_sem=r.block_recv.at[0],
        device_id=across,
        device_id_type=MESH,
    )
    pl.when(has_across)(cross_copy.start)
    r.outgoing[0] = r.blocks[jnp.where(odd, 0, jnp.maximum(load - 2, 0))]
    r.outgoing[1] = r.blocks[jnp.where(odd, 1, tail)]
    pair_copy = pltpu.make_async_remote_copy(
        src_ref=r.outgoing.at[pl.ds(0, 2)],
        dst_ref=r.moved.at[pl.ds(0, 2)],
        send_sem=r.block_send.at[1],
        recv_sem=r.block_recv.at[1],
        device_id=partner,
        device_id_type=MESH,
    )
    pair_copy.start()

    for copy in local[2:]:
        copy.wait()
    build_weights(r)
    places, final = settle_places(r, owners, own, odd, load, tail)
    build_mask(r, final)
    rank_halos(r)
    for i in range(4):

        @pl.when(jnp.logical_not(there[i]))
        def _():
            for b in range(4):
                for f in range(6):
                    r.asked_s[i, b, f] = -1

    for_sides(lambda i: lists[i ^ 1].wait_recv())
    asked = rank_asked(r)

    pl.when(has_across)(cross_copy.wait_recv)
    pair_copy.wait_recv()
    settle(r, places)

    for layer in range(2):
        recv_f = (r.recv_first, r.recv_second)[layer]
        build_faces(r)
        pick_faces(r, layer, asked)
        copies = [
            pltpu.make_async_remote_copy(
                src_ref=r.send_f.at[layer, pl.ds(4 * i, 4)],
                dst_ref=recv_f.at[pl.ds(4 * (i ^ 1), 4)],
                send_sem=r.face_send.at[layer, i],
                recv_sem=r.face_recv.at[layer, i ^ 1],
                device_id=sides[i],
                device_id_type=MESH,
            )
            for i in range(4)
        ]
        for_sides(lambda i: copies[i].start())
        for_sides(lambda i: copies[i].wait_send())
        for_sides(lambda i: copies[i ^ 1].wait_recv())

        build_lhs(r, read_halos(r, recv_f))
        convolve(r, layer)

    for_sides(lambda i: lists[i].wait_send())
    pl.when(has_across)(cross_copy.wait_send)
    pair_copy.wait_send()


def local_program(groups, owners, features, block_loads, swap_counts, neighbours, occupancy, conv_weights, norm_gains):
    any_space = pl.BlockSpec(memory_space=pl.ANY)
    return pl.pallas_call(
        functools.partial(kernel, groups, owners),
        out_shape=jax.ShapeDtypeStruct((4, 8, 8, 512), BF16),
        in_specs=[any_space] * 7,
        out_specs=pl.BlockSpec(memory_space=pltpu.VMEM),
        scratch_shapes=list(SCRATCH.values()),
        compiler_params=pltpu.CompilerParams(
            collective_id=0, has_side_effects=True, vmem_limit_bytes=60 * 1024 * 1024
        ),
    )(
        features.reshape(4, 64, 512),
        block_loads,
        swap_counts,
        neighbours,
        occupancy,
        conv_weights,
        norm_gains,
    )


def solution(mesh):
    groups, owners = mesh.shape["grp"], mesh.shape["curve"]
    return jax.shard_map(
        functools.partial(local_program, groups, owners),
        mesh=mesh,
        in_specs=(
            P(("grp", "curve"), None, None, None),
            P(("grp", "curve")),
            P("grp", None, None),
            P(("grp", "curve"), None),
            P(("grp", "curve"), None),
            P(),
            P(),
        ),
        out_specs=P(("grp", "curve"), None, None, None),
        check_vma=False,
    )
```

```python
import functools
import types

import jax
import jax.numpy as jnp
from jax import lax
from jax.experimental import pallas as pl
from jax.experimental.pallas import tpu as pltpu
from jax.sharding import PartitionSpec as P

F32 = jnp.float32
BF16 = jnp.bfloat16
I32 = jnp.int32
MESH = pl.DeviceIdType.MESH

SCRATCH = dict(
    blocks=pltpu.VMEM((4, 64, 512), BF16),
    moved=pltpu.VMEM((3, 64, 512), BF16),
    outgoing=pltpu.VMEM((3, 64, 512), BF16),
    loads_s=pltpu.SMEM((1,), I32),
    swaps_s=pltpu.SMEM((1, 2, 32), I32),
    nbrs_s=pltpu.SMEM((4, 6), I32),
    asked_s=pltpu.SMEM((4, 4, 6), I32),
    own_at=pltpu.SMEM((4, 6), I32),
    far_at=pltpu.SMEM((4, 6), I32),
    kind_at=pltpu.SMEM((4, 6), I32),
    occ_v=pltpu.VMEM((4, 512), I32),
    w_v=pltpu.VMEM((2, 27, 64, 64), BF16),
    g_v=pltpu.VMEM((2, 64), F32),
    banded=pltpu.VMEM((2, 768, 384), BF16),
    mask=pltpu.VMEM((256, 512), F32),
    nat=pltpu.VMEM((4, 256, 128), F32),
    faces=pltpu.VMEM((24, 32, 128), BF16),
    send_f=pltpu.VMEM((2, 16, 32, 128), BF16),
    recv_first=pltpu.VMEM((16, 32, 128), BF16),
    recv_second=pltpu.VMEM((16, 32, 128), BF16),
    lhs=pltpu.VMEM((3, 256, 640), BF16),
    x_lhs=pltpu.VMEM((2, 3, 32, 640), BF16),
    y_lhs=pltpu.VMEM((2, 32, 640), BF16),
    z_lhs=pltpu.VMEM((3, 256, 128), BF16),
    acc=pltpu.VMEM((4, 256, 128), F32),
    y_add=pltpu.VMEM((2, 4, 4, 8, 128), F32),
    in_sems=pltpu.SemaphoreType.DMA((7,)),
    list_send=pltpu.SemaphoreType.DMA((4,)),
    list_recv=pltpu.SemaphoreType.DMA((4,)),
    block_send=pltpu.SemaphoreType.DMA((2,)),
    block_recv=pltpu.SemaphoreType.DMA((2,)),
    face_send=pltpu.SemaphoreType.DMA((2, 4)),
    face_recv=pltpu.SemaphoreType.DMA((2, 4)),
)
OPERANDS = ("feat", "loads", "swaps", "nbrs", "occ", "wts", "gains", "out")


def lanes_low():
    return lax.broadcasted_iota(I32, (8, 128), 1) < 64


def half_turn(tile):
    return pltpu.roll(tile, 64, 1)


def widen(tiles, low_side, high_side):
    low = lanes_low()
    turned = [half_turn(t) for t in tiles]
    out = [jnp.where(low, low_side, turned[0])]
    for t in range(1, 4):
        out.append(jnp.where(low, turned[t - 1], turned[t]))
    out.append(jnp.where(low, turned[3], high_side))
    return jnp.concatenate(out, axis=1)


def build_weights(r):
    zero_w = jnp.zeros((64, 64), BF16)
    for layer in range(2):
        for dx in range(3):
            for dy in range(3):
                w = [r.w_v[layer, dx * 9 + dy * 3 + dz] for dz in range(3)]
                rows = [(w[0], zero_w), (w[1], w[0]), (w[2], w[1]), (zero_w, w[2])]
                for zi in range(4):
                    r.banded[layer, pl.ds((dy * 4 + zi) * 64, 64), pl.ds(dx * 128, 128)] = (
                        jnp.concatenate(rows[zi], axis=1)
                    )


def settle_places(r, owners, own, odd, load, tail):
    swap = r.swaps_s[0, 0, own - lax.rem(own, 2)]
    flow_in = jnp.where(own > 0, r.swaps_s[0, 1, jnp.maximum(own - 1, 0)], 0)
    flow_out = jnp.where(own < owners - 1, r.swaps_s[0, 1, own], 0)
    first_load = load + jnp.where(odd, swap, -swap)
    came = jnp.maximum(flow_in, 0)
    dropped = jnp.maximum(-flow_in, 0)
    middle = first_load - dropped - jnp.maximum(flow_out, 0)
    taken = jnp.maximum(-flow_out, 0)
    final = first_load + flow_in - flow_out
    came_at = jnp.where(odd, jnp.where(swap > 0, 4, jnp.where(swap < 0, 0, 5)), 6)
    taken_at = jnp.where(odd, 6, jnp.where(swap > 0, tail, jnp.where(swap < 0, 5, 4)))
    places = []
    for j in range(4):
        i = j - came + dropped
        even_at = jnp.where(i < load - jnp.maximum(swap, 0), i, 4)
        odd_at = jnp.where((swap > 0) & (i == 0), 5, i - swap)
        kept_at = jnp.where(odd, odd_at, even_at)
        at = jnp.where(
            j < came,
            came_at,
            jnp.where(j < came + middle, kept_at, jnp.where(j < came + middle + taken, taken_at, 0)),
        )
        places.append(jnp.clip(at, 0, 6))
    return places, final


def build_mask(r, final):
    block_no = lax.broadcasted_iota(I32, (4, 512), 0)
    occupied = jnp.where((block_no < final) & (r.occ_v[...] > 0), 1.0, 0.0).astype(F32)
    lane3 = lax.broadcasted_iota(I32, (4, 8, 128), 2)
    sub3 = lax.broadcasted_iota(I32, (4, 8, 128), 1)
    strips = []
    for x in range(8):
        strip = occupied[:, 128 * (x // 2) : 128 * (x // 2) + 128]
        wide = jnp.broadcast_to(strip[:, None, :], (4, 8, 128))
        pick = (lane3 // 8) == (sub3 + 8 * (x % 2))
        strips.append(jnp.where(pick, wide, 0.0).reshape(32, 128))
    strips = jnp.concatenate(strips, axis=0).astype(BF16)
    spread = jnp.where(
        lax.rem(lax.broadcasted_iota(I32, (128, 512), 0), 8)
        == lax.broadcasted_iota(I32, (128, 512), 1) // 64,
        1.0,
        0.0,
    ).astype(BF16)
    r.mask[...] = jnp.dot(strips, spread, preferred_element_type=F32)


def rank_halos(r):
    def rank_step(b, counts):
        counts = list(counts)
        for f in range(6):
            v = r.nbrs_s[b, f]
            s = lax.shift_right_arithmetic(v, 2)
            rank = jnp.int32(0)
            for i in range(4):
                hit = s == i + 1
                rank = jnp.where(hit, 4 * i + counts[i], rank)
                counts[i] = counts[i] + hit.astype(I32)
            r.kind_at[b, f] = s
            r.own_at[b, f] = jnp.where(v >= 0, (v & 3) * 6 + (f ^ 1), 0)
            r.far_at[b, f] = jnp.clip(rank, 0, 15)
        return tuple(counts)

    lax.fori_loop(0, 4, rank_step, (jnp.int32(0),) * 4)


def rank_asked(r):
    def ask_step(b, state):
        state = [list(row) for row in state]
        for f in range(6):
            for i in range(4):
                v = r.asked_s[i, b, f]
                count = state[i][4]
                hit = lax.shift_right_arithmetic(v, 2) == (i ^ 1) + 1
                face = (v & 3) * 6 + (f ^ 1)
                for j in range(4):
                    state[i][j] = jnp.where(hit & (count == j), face, state[i][j])
                state[i][4] = count + hit.astype(I32)
        return tuple(tuple(row) for row in state)

    return lax.fori_loop(0, 4, ask_step, ((jnp.int32(0),) * 5,) * 4)


def settle(r, places):
    for j in range(4):
        mine = r.blocks[jnp.minimum(places[j], 3)].astype(F32)
        other = r.moved[jnp.maximum(places[j] - 4, 0)].astype(F32)
        block = jnp.where(places[j] < 4, mine, other)
        for x in range(8):
            rows = pl.ds(x * 32 + j * 8, 8)
            kept = jnp.where(r.mask[rows, :] > 0.5, block[8 * x : 8 * x + 8], 0.0)
            for t in range(4):
                r.nat[t, rows, :] = kept[:, 128 * t : 128 * t + 128]


def build_faces(r):
    low = lanes_low()
    for b in range(4):
        for f in range(2):
            face = [r.nat[t, pl.ds(7 * f * 32 + b * 8, 8), :] for t in range(4)]
            r.faces[b * 6 + f] = jnp.concatenate(face, axis=0).astype(BF16)
            face = [r.nat[t, pl.ds(b * 8 + 7 * f, 8, stride=32), :] for t in range(4)]
            r.faces[b * 6 + 2 + f] = jnp.concatenate(face, axis=0).astype(BF16)
        for f in range(2):
            face = []
            for x in range(4):
                here = r.nat[3 * f, pl.ds(x * 32 + b * 8, 8), :]
                there = r.nat[3 * f, pl.ds((x + 4) * 32 + b * 8, 8), :]
                if f == 0:
                    there = half_turn(there)
                else:
                    here = half_turn(here)
                face.append(jnp.where(low, here, there))
            r.faces[b * 6 + 4 + f] = jnp.concatenate(face, axis=0).astype(BF16)


def pick_faces(r, layer, asked):
    for i in range(4):
        for j in range(4):
            r.send_f[layer, 4 * i + j] = r.faces[asked[i][j]]


def read_halos(r, recv_f):
    def halo(b, f):
        kind = r.kind_at[b, f]
        mine = r.faces[r.own_at[b, f]].astype(F32)
        far = recv_f[r.far_at[b, f]].astype(F32)
        zero = jnp.zeros((32, 128), F32)
        both = jnp.where(kind == 0, mine, jnp.where(kind > 0, far, zero))
        return [both[8 * t : 8 * t + 8] for t in range(4)]

    return [[halo(b, f) for f in range(6)] for b in range(4)]


def shifted_rows(tile):
    sub = lax.broadcasted_iota(I32, tile.shape, 0)
    return (
        jnp.where(sub == 0, 0.0, pltpu.roll(tile, 1, 0)),
        tile,
        jnp.where(sub == 7, 0.0, pltpu.roll(tile, 7, 0)),
    )


def put_pair(ref, at, row, tiles):
    ref[at + (pl.ds(row, 16), slice(None))] = jnp.concatenate(tiles, axis=0).astype(BF16)


def build_lhs(r):
    none8 = jnp.zeros((8, 128), F32)
    for x in range(8):
        for pair in range(2):
            row = x * 32 + pair * 16
            parts = []
            for b in (2 * pair, 2 * pair + 1):
                tiles = [r.nat[t, pl.ds(x * 32 + b * 8, 8), :] for t in range(4)]
                parts.append(shifted_rows(widen(tiles, none8, none8)))
            for dy in range(3):
                put_pair(r.lhs, (dy,), row, [part[dy] for part in parts])


def over_dx(three):
    rim = jnp.zeros((32, 128), F32)
    return (
        three[:, 128:256]
        + jnp.concatenate([rim, three[0:224, 0:128]], axis=0)
        + jnp.concatenate([three[32:256, 256:384], rim], axis=0)
    )


def convolve_own(r, layer):
    for k in range(4):
        window = jnp.concatenate([r.lhs[dy, :, pl.ds(128 * k, 256)] for dy in range(3)], axis=1)
        three = jnp.dot(window, r.banded[layer], preferred_element_type=F32)
        r.acc[k] = over_dx(three)


def add_halos(r, layer, halos):
    none8 = jnp.zeros((8, 128), F32)
    low = lanes_low()
    for f in range(2):
        for pair in range(2):
            wide = [widen(halos[b][f], none8, none8) for b in (2 * pair, 2 * pair + 1)]
            parts = [shifted_rows(tile) for tile in wide]
            for dy in range(3):
                put_pair(r.x_lhs, (f, dy), 16 * pair, [part[dy] for part in parts])
            wide = [widen(halos[b][2 + f], none8, none8) for b in (2 * pair, 2 * pair + 1)]
            put_pair(r.y_lhs, (f,), 16 * pair, wide)
    for pair in range(2):
        parts = [[None] * 2 for _ in range(8)]
        for i, b in enumerate((2 * pair, 2 * pair + 1)):
            for x in range(4):
                first, last = halos[b][4][x], halos[b][5][x]
                parts[x][i] = shifted_rows(jnp.where(low, first, half_turn(last)))
                parts[x + 4][i] = shifted_rows(jnp.where(low, half_turn(first), last))
        for x in range(8):
            for dy in range(3):
                put_pair(r.z_lhs, (dy,), x * 32 + 16 * pair, [part[dy] for part in parts[x]])

    for f in range(2):
        window = jnp.concatenate(
            [
                jnp.concatenate([r.x_lhs[f, dy, :, pl.ds(128 * k, 256)] for dy in range(3)], axis=1)
                for k in range(4)
            ],
            axis=0,
        )
        part = jnp.dot(
            window, r.banded[layer, :, pl.ds(256 * f, 128)], preferred_element_type=F32
        )
        for k in range(4):
            rows = pl.ds(224 * f, 32)
            r.acc[k, rows, :] = r.acc[k, rows, :] + part[32 * k : 32 * k + 32]

        window = jnp.concatenate([r.y_lhs[f, :, pl.ds(128 * k, 256)] for k in range(4)], axis=0)
        part = jnp.dot(
            window, r.banded[layer, pl.ds(512 * f, 256), :], preferred_element_type=F32
        )
        for k in range(4):
            for b in range(4):
                tile = part[32 * k + 8 * b : 32 * k + 8 * b + 8]
                r.y_add[f, k, b] = (
                    shifted_rows(tile[:, 0:128])[0]
                    + tile[:, 128:256]
                    + shifted_rows(tile[:, 256:384])[2]
                )

    window = jnp.concatenate([r.z_lhs[dy] for dy in range(3)], axis=1)
    ends = jnp.concatenate(
        [r.banded[layer, pl.ds(dy * 256 + at, 64), :] for dy in range(3) for at in (0, 192)], axis=0
    )
    z_add = over_dx(jnp.dot(window, ends, preferred_element_type=F32))

    sub = lax.broadcasted_iota(I32, (8, 128), 0)
    for k in range(4):
        for x in range(8):
            for b in range(4):
                rows = pl.ds(x * 32 + b * 8, 8)
                first = jnp.broadcast_to(r.y_add[0, k, b, pl.ds(x, 1), :], (8, 128))
                last = jnp.broadcast_to(r.y_add[1, k, b, pl.ds(x, 1), :], (8, 128))
                tile = r.acc[k, rows, :]
                tile = tile + jnp.where(sub == 0, first, jnp.where(sub == 7, last, 0.0))
                side = z_add[x * 32 + b * 8 : x * 32 + b * 8 + 8]
                if k == 0:
                    tile = tile + jnp.where(low, side, 0.0)
                if k == 3:
                    tile = tile + jnp.where(low, 0.0, side)
                r.acc[k, rows, :] = tile


def finish(r, layer):
    group_lane = lax.broadcasted_iota(I32, (256, 128), 1) // 64
    group_row = lax.rem(lax.broadcasted_iota(I32, (256, 128), 0), 128) // 64
    averager = jnp.where(group_lane == group_row, 1.0 / 64.0, 0.0).astype(BF16)
    gain = r.g_v[pl.ds(layer, 1), :]
    gain = jnp.concatenate([gain, gain], axis=1)
    for k in range(4):
        total = r.acc[k]
        square = total * total
        coarse = square.astype(BF16)
        fine = (square - coarse.astype(F32)).astype(BF16)
        mean = jnp.dot(
            jnp.concatenate([coarse, fine], axis=1), averager, preferred_element_type=F32
        )
        scaled = total * lax.rsqrt(mean + 1e-5) * gain
        keep = r.mask[:, pl.ds(128 * k, 128)] > 0.5
        done = jnp.where(keep, jnp.maximum(scaled, 0.0), 0.0)
        if layer == 0:
            r.nat[k] = done
        else:
            cells = done.reshape(8, 4, 8, 128)
            for b in range(4):
                r.out[b, :, :, pl.ds(128 * k, 128)] = cells[:, b].astype(BF16)


def kernel(groups, owners, *refs):
    r = types.SimpleNamespace(**dict(zip(OPERANDS + tuple(SCRATCH), refs)))
    grp = lax.axis_index("grp")
    own = lax.axis_index("curve")
    odd = lax.rem(own, 2) == 1
    sides = (
        (grp, jnp.maximum(own - 1, 0)),
        (grp, jnp.minimum(own + 1, owners - 1)),
        (jnp.maximum(grp - 1, 0), own),
        (jnp.minimum(grp + 1, groups - 1), own),
    )
    there = (own > 0, own < owners - 1, grp > 0, grp < groups - 1)

    def for_sides(step):
        for i in range(4):
            pl.when(there[i])(functools.partial(step, i))

    local = [
        pltpu.make_async_copy(source, target, r.in_sems.at[i])
        for i, (source, target) in enumerate(
            (
                (r.feat, r.blocks),
                (r.loads, r.loads_s),
                (r.swaps, r.swaps_s),
                (r.nbrs, r.nbrs_s),
                (r.occ, r.occ_v),
                (r.wts, r.w_v),
                (r.gains, r.g_v),
            )
        )
    ]
    for copy in local:
        copy.start()

    barrier = pltpu.get_barrier_semaphore()
    for_sides(
        lambda i: pl.semaphore_signal(barrier, inc=1, device_id=sides[i], device_id_type=MESH)
    )
    pl.semaphore_wait(barrier, sum(flag.astype(I32) for flag in there))

    lists = [
        pltpu.make_async_remote_copy(
            src_ref=r.nbrs,
            dst_ref=r.asked_s.at[i ^ 1],
            send_sem=r.list_send.at[i],
            recv_sem=r.list_recv.at[i ^ 1],
            device_id=sides[i],
            device_id_type=MESH,
        )
        for i in range(4)
    ]
    for_sides(lambda i: lists[i].start())

    local[1].wait()
    local[0].wait()
    load = r.loads_s[0]
    tail = jnp.maximum(load - 1, 0)
    r.outgoing[2] = r.blocks[jnp.where(odd, tail, 0)]
    partner = (grp, own + 1 - 2 * lax.rem(own, 2))
    across = (grp, jnp.clip(own - 1 + 2 * lax.rem(own, 2), 0, owners - 1))
    has_across = (own > 0) & (own < owners - 1)
    cross_copy = pltpu.make_async_remote_copy(
        src_ref=r.outgoing.at[pl.ds(2, 1)],
        dst_ref=r.moved.at[pl.ds(2, 1)],
        send_sem=r.block_send.at[0],
        recv_sem=r.block_recv.at[0],
        device_id=across,
        device_id_type=MESH,
    )
    pl.when(has_across)(cross_copy.start)
    r.outgoing[0] = r.blocks[jnp.where(odd, 0, jnp.maximum(load - 2, 0))]
    r.outgoing[1] = r.blocks[jnp.where(odd, 1, tail)]
    pair_copy = pltpu.make_async_remote_copy(
        src_ref=r.outgoing.at[pl.ds(0, 2)],
        dst_ref=r.moved.at[pl.ds(0, 2)],
        send_sem=r.block_send.at[1],
        recv_sem=r.block_recv.at[1],
        device_id=partner,
        device_id_type=MESH,
    )
    pair_copy.start()

    for copy in local[2:]:
        copy.wait()
    build_weights(r)
    places, final = settle_places(r, owners, own, odd, load, tail)
    build_mask(r, final)
    rank_halos(r)
    for i in range(4):

        @pl.when(jnp.logical_not(there[i]))
        def _():
            for b in range(4):
                for f in range(6):
                    r.asked_s[i, b, f] = -1

    for_sides(lambda i: lists[i ^ 1].wait_recv())
    asked = rank_asked(r)

    pl.when(has_across)(cross_copy.wait_recv)
    pair_copy.wait_recv()
    settle(r, places)

    sent = []
    for layer in range(2):
        recv_f = (r.recv_first, r.recv_second)[layer]
        build_faces(r)
        pick_faces(r, layer, asked)
        copies = [
            pltpu.make_async_remote_copy(
                src_ref=r.send_f.at[layer, pl.ds(4 * i, 4)],
                dst_ref=recv_f.at[pl.ds(4 * (i ^ 1), 4)],
                send_sem=r.face_send.at[layer, i],
                recv_sem=r.face_recv.at[layer, i ^ 1],
                device_id=sides[i],
                device_id_type=MESH,
            )
            for i in range(4)
        ]
        for_sides(lambda i: copies[i].start())

        build_lhs(r)
        convolve_own(r, layer)
        for_sides(lambda i: copies[i ^ 1].wait_recv())
        add_halos(r, layer, read_halos(r, recv_f))
        finish(r, layer)
        sent += copies

    for_sides(lambda i: lists[i].wait_send())
    for_sides(lambda i: sent[i].wait_send())
    for_sides(lambda i: sent[4 + i].wait_send())
    pl.when(has_across)(cross_copy.wait_send)
    pair_copy.wait_send()


def local_program(groups, owners, features, block_loads, swap_counts, neighbours, occupancy, conv_weights, norm_gains):
    in_hbm = pl.BlockSpec(memory_space=pltpu.HBM)
    return pl.pallas_call(
        functools.partial(kernel, groups, owners),
        out_shape=jax.ShapeDtypeStruct((4, 8, 8, 512), BF16),
        in_specs=[in_hbm] * 7,
        out_specs=pl.BlockSpec(memory_space=pltpu.VMEM),
        scratch_shapes=list(SCRATCH.values()),
        compiler_params=pltpu.CompilerParams(
            collective_id=0, has_side_effects=True, vmem_limit_bytes=32 * 1024 * 1024
        ),
    )(
        features.reshape(4, 64, 512),
        block_loads,
        swap_counts,
        neighbours,
        occupancy,
        conv_weights,
        norm_gains,
    )


def solution(mesh):
    groups, owners = mesh.shape["grp"], mesh.shape["curve"]
    return jax.shard_map(
        functools.partial(local_program, groups, owners),
        mesh=mesh,
        in_specs=(
            P(("grp", "curve"), None, None, None),
            P(("grp", "curve")),
            P("grp", None, None),
            P(("grp", "curve"), None),
            P(("grp", "curve"), None),
            P(),
            P(),
        ),
        out_specs=P(("grp", "curve"), None, None, None),
        check_vma=False,
    )
```

```python
import functools
import types

import jax
import jax.numpy as jnp
from jax import lax
from jax.experimental import pallas as pl
from jax.experimental.pallas import tpu as pltpu
from jax.sharding import PartitionSpec as P

F32 = jnp.float32
BF16 = jnp.bfloat16
I32 = jnp.int32
MESH = pl.DeviceIdType.MESH

SCRATCH = dict(
    blocks=pltpu.VMEM((4, 64, 512), BF16),
    moved=pltpu.VMEM((3, 64, 512), BF16),
    outgoing=pltpu.VMEM((3, 64, 512), BF16),
    swaps_s=pltpu.SMEM((1, 2, 32), I32),
    nbrs_s=pltpu.SMEM((4, 6), I32),
    asked_s=pltpu.SMEM((4, 4, 6), I32),
    own_at=pltpu.SMEM((4, 6), I32),
    far_at=pltpu.SMEM((4, 6), I32),
    kind_at=pltpu.SMEM((4, 6), I32),
    occ_v=pltpu.VMEM((4, 512), I32),
    w_v=pltpu.VMEM((2, 27, 64, 64), BF16),
    g_v=pltpu.VMEM((2, 64), F32),
    banded=pltpu.VMEM((2, 768, 384), BF16),
    mask=pltpu.VMEM((256, 512), F32),
    nat=pltpu.VMEM((4, 256, 128), F32),
    faces=pltpu.VMEM((24, 32, 128), BF16),
    send_f=pltpu.VMEM((2, 16, 32, 128), BF16),
    recv_first=pltpu.VMEM((16, 32, 128), BF16),
    recv_second=pltpu.VMEM((16, 32, 128), BF16),
    lhs=pltpu.VMEM((3, 256, 640), BF16),
    x_lhs=pltpu.VMEM((2, 3, 32, 640), BF16),
    y_lhs=pltpu.VMEM((2, 32, 640), BF16),
    z_lhs=pltpu.VMEM((3, 256, 128), BF16),
    acc=pltpu.VMEM((4, 256, 128), F32),
    y_add=pltpu.VMEM((2, 4, 4, 8, 128), F32),
    in_sems=pltpu.SemaphoreType.DMA((6,)),
    list_send=pltpu.SemaphoreType.DMA((4,)),
    list_recv=pltpu.SemaphoreType.DMA((4,)),
    block_send=pltpu.SemaphoreType.DMA((2,)),
    block_recv=pltpu.SemaphoreType.DMA((2,)),
    face_send=pltpu.SemaphoreType.DMA((2, 4)),
    face_recv=pltpu.SemaphoreType.DMA((2, 4)),
)
OPERANDS = ("loads", "feat", "swaps", "nbrs", "occ", "wts", "gains", "out")


def lanes_low():
    return lax.broadcasted_iota(I32, (8, 128), 1) < 64


def half_turn(tile):
    return pltpu.roll(tile, 64, 1)


def widen(tiles, low_side, high_side):
    low = lanes_low()
    turned = [half_turn(t) for t in tiles]
    out = [jnp.where(low, low_side, turned[0])]
    for t in range(1, 4):
        out.append(jnp.where(low, turned[t - 1], turned[t]))
    out.append(jnp.where(low, turned[3], high_side))
    return jnp.concatenate(out, axis=1)


def build_weights(r):
    zero_w = jnp.zeros((64, 64), BF16)
    for layer in range(2):
        for dx in range(3):
            for dy in range(3):
                w = [r.w_v[layer, dx * 9 + dy * 3 + dz] for dz in range(3)]
                rows = [(w[0], zero_w), (w[1], w[0]), (w[2], w[1]), (zero_w, w[2])]
                for zi in range(4):
                    r.banded[layer, pl.ds((dy * 4 + zi) * 64, 64), pl.ds(dx * 128, 128)] = (
                        jnp.concatenate(rows[zi], axis=1)
                    )


def settle_places(r, owners, own, odd, load, tail):
    swap = r.swaps_s[0, 0, own - lax.rem(own, 2)]
    flow_in = jnp.where(own > 0, r.swaps_s[0, 1, jnp.maximum(own - 1, 0)], 0)
    flow_out = jnp.where(own < owners - 1, r.swaps_s[0, 1, own], 0)
    first_load = load + jnp.where(odd, swap, -swap)
    came = jnp.maximum(flow_in, 0)
    dropped = jnp.maximum(-flow_in, 0)
    middle = first_load - dropped - jnp.maximum(flow_out, 0)
    taken = jnp.maximum(-flow_out, 0)
    final = first_load + flow_in - flow_out
    came_at = jnp.where(odd, jnp.where(swap > 0, 4, jnp.where(swap < 0, 0, 5)), 6)
    taken_at = jnp.where(odd, 6, jnp.where(swap > 0, tail, jnp.where(swap < 0, 5, 4)))
    places = []
    for j in range(4):
        i = j - came + dropped
        even_at = jnp.where(i < load - jnp.maximum(swap, 0), i, 4)
        odd_at = jnp.where((swap > 0) & (i == 0), 5, i - swap)
        kept_at = jnp.where(odd, odd_at, even_at)
        at = jnp.where(
            j < came,
            came_at,
            jnp.where(j < came + middle, kept_at, jnp.where(j < came + middle + taken, taken_at, 0)),
        )
        places.append(jnp.clip(at, 0, 6))
    return places, final


def build_mask(r, final):
    block_no = lax.broadcasted_iota(I32, (4, 512), 0)
    occupied = jnp.where((block_no < final) & (r.occ_v[...] > 0), 1.0, 0.0).astype(F32)
    lane3 = lax.broadcasted_iota(I32, (4, 8, 128), 2)
    sub3 = lax.broadcasted_iota(I32, (4, 8, 128), 1)
    strips = []
    for x in range(8):
        strip = occupied[:, 128 * (x // 2) : 128 * (x // 2) + 128]
        wide = jnp.broadcast_to(strip[:, None, :], (4, 8, 128))
        pick = (lane3 // 8) == (sub3 + 8 * (x % 2))
        strips.append(jnp.where(pick, wide, 0.0).reshape(32, 128))
    strips = jnp.concatenate(strips, axis=0).astype(BF16)
    spread = jnp.where(
        lax.rem(lax.broadcasted_iota(I32, (128, 512), 0), 8)
        == lax.broadcasted_iota(I32, (128, 512), 1) // 64,
        1.0,
        0.0,
    ).astype(BF16)
    r.mask[...] = jnp.dot(strips, spread, preferred_element_type=F32)


def rank_halos(r):
    def rank_step(b, counts):
        counts = list(counts)
        for f in range(6):
            v = r.nbrs_s[b, f]
            s = lax.shift_right_arithmetic(v, 2)
            rank = jnp.int32(0)
            for i in range(4):
                hit = s == i + 1
                rank = jnp.where(hit, 4 * i + counts[i], rank)
                counts[i] = counts[i] + hit.astype(I32)
            r.kind_at[b, f] = s
            r.own_at[b, f] = jnp.where(v >= 0, (v & 3) * 6 + (f ^ 1), 0)
            r.far_at[b, f] = jnp.clip(rank, 0, 15)
        return tuple(counts)

    lax.fori_loop(0, 4, rank_step, (jnp.int32(0),) * 4)


def rank_asked(r):
    def ask_step(b, state):
        state = [list(row) for row in state]
        for f in range(6):
            for i in range(4):
                v = r.asked_s[i, b, f]
                count = state[i][4]
                hit = lax.shift_right_arithmetic(v, 2) == (i ^ 1) + 1
                face = (v & 3) * 6 + (f ^ 1)
                for j in range(4):
                    state[i][j] = jnp.where(hit & (count == j), face, state[i][j])
                state[i][4] = count + hit.astype(I32)
        return tuple(tuple(row) for row in state)

    return lax.fori_loop(0, 4, ask_step, ((jnp.int32(0),) * 5,) * 4)


def settle(r, places):
    for j in range(4):
        mine = r.blocks[jnp.minimum(places[j], 3)].astype(F32)
        other = r.moved[jnp.maximum(places[j] - 4, 0)].astype(F32)
        block = jnp.where(places[j] < 4, mine, other)
        for x in range(8):
            rows = pl.ds(x * 32 + j * 8, 8)
            kept = jnp.where(r.mask[rows, :] > 0.5, block[8 * x : 8 * x + 8], 0.0)
            for t in range(4):
                r.nat[t, rows, :] = kept[:, 128 * t : 128 * t + 128]


def build_faces(r):
    low = lanes_low()
    for b in range(4):
        for f in range(2):
            face = [r.nat[t, pl.ds(7 * f * 32 + b * 8, 8), :] for t in range(4)]
            r.faces[b * 6 + f] = jnp.concatenate(face, axis=0).astype(BF16)
            face = [r.nat[t, pl.ds(b * 8 + 7 * f, 8, stride=32), :] for t in range(4)]
            r.faces[b * 6 + 2 + f] = jnp.concatenate(face, axis=0).astype(BF16)
        for f in range(2):
            face = []
            for x in range(4):
                here = r.nat[3 * f, pl.ds(x * 32 + b * 8, 8), :]
                there = r.nat[3 * f, pl.ds((x + 4) * 32 + b * 8, 8), :]
                if f == 0:
                    there = half_turn(there)
                else:
                    here = half_turn(here)
                face.append(jnp.where(low, here, there))
            r.faces[b * 6 + 4 + f] = jnp.concatenate(face, axis=0).astype(BF16)


def pick_faces(r, layer, asked):
    for i in range(4):
        for j in range(4):
            r.send_f[layer, 4 * i + j] = r.faces[asked[i][j]]


def read_halos(r, recv_f):
    def halo(b, f):
        kind = r.kind_at[b, f]
        mine = r.faces[r.own_at[b, f]].astype(F32)
        far = recv_f[r.far_at[b, f]].astype(F32)
        zero = jnp.zeros((32, 128), F32)
        both = jnp.where(kind == 0, mine, jnp.where(kind > 0, far, zero))
        return [both[8 * t : 8 * t + 8] for t in range(4)]

    return [[halo(b, f) for f in range(6)] for b in range(4)]


def shifted_rows(tile):
    sub = lax.broadcasted_iota(I32, tile.shape, 0)
    return (
        jnp.where(sub == 0, 0.0, pltpu.roll(tile, 1, 0)),
        tile,
        jnp.where(sub == 7, 0.0, pltpu.roll(tile, 7, 0)),
    )


def put_pair(ref, at, row, tiles):
    ref[at + (pl.ds(row, 16), slice(None))] = jnp.concatenate(tiles, axis=0).astype(BF16)


def build_lhs(r):
    none8 = jnp.zeros((8, 128), F32)
    for x in range(8):
        for pair in range(2):
            row = x * 32 + pair * 16
            parts = []
            for b in (2 * pair, 2 * pair + 1):
                tiles = [r.nat[t, pl.ds(x * 32 + b * 8, 8), :] for t in range(4)]
                parts.append(shifted_rows(widen(tiles, none8, none8)))
            for dy in range(3):
                put_pair(r.lhs, (dy,), row, [part[dy] for part in parts])


def over_dx(three):
    rim = jnp.zeros((32, 128), F32)
    return (
        three[:, 128:256]
        + jnp.concatenate([rim, three[0:224, 0:128]], axis=0)
        + jnp.concatenate([three[32:256, 256:384], rim], axis=0)
    )


def convolve_own(r, layer):
    for k in range(4):
        window = jnp.concatenate([r.lhs[dy, :, pl.ds(128 * k, 256)] for dy in range(3)], axis=1)
        three = jnp.dot(window, r.banded[layer], preferred_element_type=F32)
        r.acc[k] = over_dx(three)


def add_halos(r, layer, halos):
    none8 = jnp.zeros((8, 128), F32)
    low = lanes_low()
    for f in range(2):
        for pair in range(2):
            wide = [widen(halos[b][f], none8, none8) for b in (2 * pair, 2 * pair + 1)]
            parts = [shifted_rows(tile) for tile in wide]
            for dy in range(3):
                put_pair(r.x_lhs, (f, dy), 16 * pair, [part[dy] for part in parts])
            wide = [widen(halos[b][2 + f], none8, none8) for b in (2 * pair, 2 * pair + 1)]
            put_pair(r.y_lhs, (f,), 16 * pair, wide)
    for pair in range(2):
        parts = [[None] * 2 for _ in range(8)]
        for i, b in enumerate((2 * pair, 2 * pair + 1)):
            for x in range(4):
                first, last = halos[b][4][x], halos[b][5][x]
                parts[x][i] = shifted_rows(jnp.where(low, first, half_turn(last)))
                parts[x + 4][i] = shifted_rows(jnp.where(low, half_turn(first), last))
        for x in range(8):
            for dy in range(3):
                put_pair(r.z_lhs, (dy,), x * 32 + 16 * pair, [part[dy] for part in parts[x]])

    for f in range(2):
        window = jnp.concatenate(
            [
                jnp.concatenate([r.x_lhs[f, dy, :, pl.ds(128 * k, 256)] for dy in range(3)], axis=1)
                for k in range(4)
            ],
            axis=0,
        )
        part = jnp.dot(
            window, r.banded[layer, :, pl.ds(256 * f, 128)], preferred_element_type=F32
        )
        for k in range(4):
            rows = pl.ds(224 * f, 32)
            r.acc[k, rows, :] = r.acc[k, rows, :] + part[32 * k : 32 * k + 32]

        window = jnp.concatenate([r.y_lhs[f, :, pl.ds(128 * k, 256)] for k in range(4)], axis=0)
        part = jnp.dot(
            window, r.banded[layer, pl.ds(512 * f, 256), :], preferred_element_type=F32
        )
        for k in range(4):
            for b in range(4):
                tile = part[32 * k + 8 * b : 32 * k + 8 * b + 8]
                r.y_add[f, k, b] = (
                    shifted_rows(tile[:, 0:128])[0]
                    + tile[:, 128:256]
                    + shifted_rows(tile[:, 256:384])[2]
                )

    window = jnp.concatenate([r.z_lhs[dy] for dy in range(3)], axis=1)
    ends = jnp.concatenate(
        [r.banded[layer, pl.ds(dy * 256 + at, 64), :] for dy in range(3) for at in (0, 192)], axis=0
    )
    z_add = over_dx(jnp.dot(window, ends, preferred_element_type=F32))

    sub = lax.broadcasted_iota(I32, (8, 128), 0)
    for k in range(4):
        for x in range(8):
            for b in range(4):
                rows = pl.ds(x * 32 + b * 8, 8)
                first = jnp.broadcast_to(r.y_add[0, k, b, pl.ds(x, 1), :], (8, 128))
                last = jnp.broadcast_to(r.y_add[1, k, b, pl.ds(x, 1), :], (8, 128))
                tile = r.acc[k, rows, :]
                tile = tile + jnp.where(sub == 0, first, jnp.where(sub == 7, last, 0.0))
                side = z_add[x * 32 + b * 8 : x * 32 + b * 8 + 8]
                if k == 0:
                    tile = tile + jnp.where(low, side, 0.0)
                if k == 3:
                    tile = tile + jnp.where(low, 0.0, side)
                r.acc[k, rows, :] = tile


def finish(r, layer):
    group_lane = lax.broadcasted_iota(I32, (256, 128), 1) // 64
    group_row = lax.rem(lax.broadcasted_iota(I32, (256, 128), 0), 128) // 64
    averager = jnp.where(group_lane == group_row, 1.0 / 64.0, 0.0).astype(BF16)
    gain = r.g_v[pl.ds(layer, 1), :]
    gain = jnp.concatenate([gain, gain], axis=1)
    for k in range(4):
        total = r.acc[k]
        square = total * total
        coarse = square.astype(BF16)
        fine = (square - coarse.astype(F32)).astype(BF16)
        mean = jnp.dot(
            jnp.concatenate([coarse, fine], axis=1), averager, preferred_element_type=F32
        )
        scaled = total * lax.rsqrt(mean + 1e-5) * gain
        keep = r.mask[:, pl.ds(128 * k, 128)] > 0.5
        done = jnp.where(keep, jnp.maximum(scaled, 0.0), 0.0)
        if layer == 0:
            r.nat[k] = done
        else:
            cells = done.reshape(8, 4, 8, 128)
            for b in range(4):
                r.out[b, :, :, pl.ds(128 * k, 128)] = cells[:, b].astype(BF16)


def kernel(groups, owners, *refs):
    r = types.SimpleNamespace(**dict(zip(OPERANDS + tuple(SCRATCH), refs)))
    grp = lax.axis_index("grp")
    own = lax.axis_index("curve")
    odd = lax.rem(own, 2) == 1
    sides = (
        (grp, jnp.maximum(own - 1, 0)),
        (grp, jnp.minimum(own + 1, owners - 1)),
        (jnp.maximum(grp - 1, 0), own),
        (jnp.minimum(grp + 1, groups - 1), own),
    )
    there = (own > 0, own < owners - 1, grp > 0, grp < groups - 1)

    def for_sides(step):
        for i in range(4):
            pl.when(there[i])(functools.partial(step, i))

    local = [
        pltpu.make_async_copy(source, target, r.in_sems.at[i])
        for i, (source, target) in enumerate(
            (
                (r.feat, r.blocks),
                (r.swaps, r.swaps_s),
                (r.nbrs, r.nbrs_s),
                (r.occ, r.occ_v),
                (r.wts, r.w_v),
                (r.gains, r.g_v),
            )
        )
    ]
    for copy in local:
        copy.start()

    barrier = pltpu.get_barrier_semaphore()
    for_sides(
        lambda i: pl.semaphore_signal(barrier, inc=1, device_id=sides[i], device_id_type=MESH)
    )
    pl.semaphore_wait(barrier, sum(flag.astype(I32) for flag in there))

    lists = [
        pltpu.make_async_remote_copy(
            src_ref=r.nbrs,
            dst_ref=r.asked_s.at[i ^ 1],
            send_sem=r.list_send.at[i],
            recv_sem=r.list_recv.at[i ^ 1],
            device_id=sides[i],
            device_id_type=MESH,
        )
        for i in range(4)
    ]
    for_sides(lambda i: lists[i].start())

    local[0].wait()
    load = r.loads[0]
    tail = jnp.maximum(load - 1, 0)
    r.outgoing[2] = r.blocks[jnp.where(odd, tail, 0)]
    partner = (grp, own + 1 - 2 * lax.rem(own, 2))
    across = (grp, jnp.clip(own - 1 + 2 * lax.rem(own, 2), 0, owners - 1))
    has_across = (own > 0) & (own < owners - 1)
    cross_copy = pltpu.make_async_remote_copy(
        src_ref=r.outgoing.at[pl.ds(2, 1)],
        dst_ref=r.moved.at[pl.ds(2, 1)],
        send_sem=r.block_send.at[0],
        recv_sem=r.block_recv.at[0],
        device_id=across,
        device_id_type=MESH,
    )
    pl.when(has_across)(cross_copy.start)
    r.outgoing[0] = r.blocks[jnp.where(odd, 0, jnp.maximum(load - 2, 0))]
    r.outgoing[1] = r.blocks[jnp.where(odd, 1, tail)]
    pair_copy = pltpu.make_async_remote_copy(
        src_ref=r.outgoing.at[pl.ds(0, 2)],
        dst_ref=r.moved.at[pl.ds(0, 2)],
        send_sem=r.block_send.at[1],
        recv_sem=r.block_recv.at[1],
        device_id=partner,
        device_id_type=MESH,
    )
    pair_copy.start()

    for copy in local[1:]:
        copy.wait()
    build_weights(r)
    places, final = settle_places(r, owners, own, odd, load, tail)
    build_mask(r, final)
    rank_halos(r)
    for i in range(4):

        @pl.when(jnp.logical_not(there[i]))
        def _():
            for b in range(4):
                for f in range(6):
                    r.asked_s[i, b, f] = -1

    for_sides(lambda i: lists[i ^ 1].wait_recv())
    asked = rank_asked(r)

    pl.when(has_across)(cross_copy.wait_recv)
    pair_copy.wait_recv()
    settle(r, places)

    sent = []
    for layer in range(2):
        recv_f = (r.recv_first, r.recv_second)[layer]
        build_faces(r)
        pick_faces(r, layer, asked)
        copies = [
            pltpu.make_async_remote_copy(
                src_ref=r.send_f.at[layer, pl.ds(4 * i, 4)],
                dst_ref=recv_f.at[pl.ds(4 * (i ^ 1), 4)],
                send_sem=r.face_send.at[layer, i],
                recv_sem=r.face_recv.at[layer, i ^ 1],
                device_id=sides[i],
                device_id_type=MESH,
            )
            for i in range(4)
        ]
        for_sides(lambda i: copies[i].start())

        build_lhs(r)
        convolve_own(r, layer)
        for_sides(lambda i: copies[i ^ 1].wait_recv())
        add_halos(r, layer, read_halos(r, recv_f))
        finish(r, layer)
        sent += copies

    for_sides(lambda i: lists[i].wait_send())
    for_sides(lambda i: sent[i].wait_send())
    for_sides(lambda i: sent[4 + i].wait_send())
    pl.when(has_across)(cross_copy.wait_send)
    pair_copy.wait_send()


def local_program(groups, owners, features, block_loads, swap_counts, neighbours, occupancy, conv_weights, norm_gains):
    operands = (
        features.reshape(4, 64, 512),
        swap_counts,
        neighbours,
        occupancy,
        conv_weights,
        norm_gains,
    )
    in_hbm = pl.BlockSpec(memory_space=pltpu.HBM)
    return pl.pallas_call(
        functools.partial(kernel, groups, owners),
        out_shape=jax.ShapeDtypeStruct((4, 8, 8, 512), BF16),
        in_specs=[pl.BlockSpec(memory_space=pltpu.SMEM)] + [in_hbm] * 6,
        out_specs=pl.BlockSpec(memory_space=pltpu.VMEM),
        scratch_shapes=list(SCRATCH.values()),
        compiler_params=pltpu.CompilerParams(
            collective_id=0, has_side_effects=True, vmem_limit_bytes=32 * 1024 * 1024
        ),
    )(block_loads, *[pltpu.with_memory_space_constraint(operand, pltpu.HBM) for operand in operands])


def solution(mesh):
    groups, owners = mesh.shape["grp"], mesh.shape["curve"]
    return jax.shard_map(
        functools.partial(local_program, groups, owners),
        mesh=mesh,
        in_specs=(
            P(("grp", "curve"), None, None, None),
            P(("grp", "curve")),
            P("grp", None, None),
            P(("grp", "curve"), None),
            P(("grp", "curve"), None),
            P(),
            P(),
        ),
        out_specs=P(("grp", "curve"), None, None, None),
        check_vma=False,
    )
```

```python
import functools
import types

import jax
import jax.numpy as jnp
from jax import lax
from jax.experimental import pallas as pl
from jax.experimental.pallas import tpu as pltpu
from jax.sharding import PartitionSpec as P

F32 = jnp.float32
BF16 = jnp.bfloat16
I32 = jnp.int32
MESH = pl.DeviceIdType.MESH

SCRATCH = dict(
    blocks=pltpu.VMEM((4, 64, 512), BF16),
    moved=pltpu.VMEM((3, 64, 512), BF16),
    outgoing=pltpu.VMEM((3, 64, 512), BF16),
    swaps_s=pltpu.SMEM((1, 2, 32), I32),
    nbrs_s=pltpu.SMEM((4, 6), I32),
    asked_s=pltpu.SMEM((4, 4, 6), I32),
    halo_at=pltpu.SMEM((4, 6), I32),
    occ_v=pltpu.VMEM((4, 512), I32),
    w_v=pltpu.VMEM((2, 27, 64, 64), BF16),
    g_v=pltpu.VMEM((2, 64), F32),
    banded=pltpu.VMEM((2, 768, 384), BF16),
    mask=pltpu.VMEM((256, 512), F32),
    nat=pltpu.VMEM((4, 256, 128), F32),
    faces=pltpu.VMEM((24, 32, 128), BF16),
    send_f=pltpu.VMEM((2, 16, 32, 128), BF16),
    recv_first=pltpu.VMEM((41, 32, 128), BF16),
    recv_second=pltpu.VMEM((41, 32, 128), BF16),
    lhs=pltpu.VMEM((3, 256, 640), BF16),
    x_lhs=pltpu.VMEM((2, 32, 640), BF16),
    y_lhs=pltpu.VMEM((2, 32, 640), BF16),
    z_lhs=pltpu.VMEM((3, 256, 128), BF16),
    acc=pltpu.VMEM((4, 256, 128), F32),
    y_add=pltpu.VMEM((2, 4, 4, 8, 128), F32),
    in_sems=pltpu.SemaphoreType.DMA((6,)),
    list_send=pltpu.SemaphoreType.DMA((4,)),
    list_recv=pltpu.SemaphoreType.DMA((4,)),
    block_send=pltpu.SemaphoreType.DMA((2,)),
    block_recv=pltpu.SemaphoreType.DMA((2,)),
    face_send=pltpu.SemaphoreType.DMA((2, 4)),
    face_recv=pltpu.SemaphoreType.DMA((2, 4)),
)
OPERANDS = ("loads", "feat", "swaps", "nbrs", "occ", "wts", "gains", "out")


def lanes_low():
    return lax.broadcasted_iota(I32, (8, 128), 1) < 64


def half_turn(tile):
    return pltpu.roll(tile, 64, 1)


def widen(tiles, low_side, high_side):
    low = lanes_low()
    turned = [half_turn(t) for t in tiles]
    out = [jnp.where(low, low_side, turned[0])]
    for t in range(1, 4):
        out.append(jnp.where(low, turned[t - 1], turned[t]))
    out.append(jnp.where(low, turned[3], high_side))
    return jnp.concatenate(out, axis=1)


def build_weights(r):
    zero_w = jnp.zeros((64, 64), BF16)
    for layer in range(2):
        for dx in range(3):
            for dy in range(3):
                w = [r.w_v[layer, dx * 9 + dy * 3 + dz] for dz in range(3)]
                rows = [(w[0], zero_w), (w[1], w[0]), (w[2], w[1]), (zero_w, w[2])]
                for zi in range(4):
                    r.banded[layer, pl.ds((dy * 4 + zi) * 64, 64), pl.ds(dx * 128, 128)] = (
                        jnp.concatenate(rows[zi], axis=1)
                    )


def settle_places(r, owners, own, odd, load, tail):
    swap = r.swaps_s[0, 0, own - lax.rem(own, 2)]
    flow_in = jnp.where(own > 0, r.swaps_s[0, 1, jnp.maximum(own - 1, 0)], 0)
    flow_out = jnp.where(own < owners - 1, r.swaps_s[0, 1, own], 0)
    first_load = load + jnp.where(odd, swap, -swap)
    came = jnp.maximum(flow_in, 0)
    dropped = jnp.maximum(-flow_in, 0)
    middle = first_load - dropped - jnp.maximum(flow_out, 0)
    taken = jnp.maximum(-flow_out, 0)
    final = first_load + flow_in - flow_out
    came_at = jnp.where(odd, jnp.where(swap > 0, 4, jnp.where(swap < 0, 0, 5)), 6)
    taken_at = jnp.where(odd, 6, jnp.where(swap > 0, tail, jnp.where(swap < 0, 5, 4)))
    places = []
    for j in range(4):
        i = j - came + dropped
        even_at = jnp.where(i < load - jnp.maximum(swap, 0), i, 4)
        odd_at = jnp.where((swap > 0) & (i == 0), 5, i - swap)
        kept_at = jnp.where(odd, odd_at, even_at)
        at = jnp.where(
            j < came,
            came_at,
            jnp.where(j < came + middle, kept_at, jnp.where(j < came + middle + taken, taken_at, 0)),
        )
        places.append(jnp.clip(at, 0, 6))
    return places, final


def build_mask(r, final):
    block_no = lax.broadcasted_iota(I32, (4, 512), 0)
    occupied = jnp.where((block_no < final) & (r.occ_v[...] > 0), 1.0, 0.0).astype(F32)
    lane3 = lax.broadcasted_iota(I32, (4, 8, 128), 2)
    sub3 = lax.broadcasted_iota(I32, (4, 8, 128), 1)
    strips = []
    for x in range(8):
        strip = occupied[:, 128 * (x // 2) : 128 * (x // 2) + 128]
        wide = jnp.broadcast_to(strip[:, None, :], (4, 8, 128))
        pick = (lane3 // 8) == (sub3 + 8 * (x % 2))
        strips.append(jnp.where(pick, wide, 0.0).reshape(32, 128))
    strips = jnp.concatenate(strips, axis=0).astype(BF16)
    spread = jnp.where(
        lax.rem(lax.broadcasted_iota(I32, (128, 512), 0), 8)
        == lax.broadcasted_iota(I32, (128, 512), 1) // 64,
        1.0,
        0.0,
    ).astype(BF16)
    r.mask[...] = jnp.dot(strips, spread, preferred_element_type=F32)


def rank_halos(r, odd):
    codes = (jnp.where(odd, 2, 1), jnp.where(odd, 1, 2), 3, 4)

    def rank_step(b, counts):
        counts = list(counts)
        for f in range(6):
            v = r.nbrs_s[b, f]
            s = lax.shift_right_arithmetic(v, 2)
            at = jnp.where(s == 0, 16 + (v & 3) * 6 + (f ^ 1), 40)
            for q in range(4):
                hit = s == codes[q]
                at = jnp.where(hit, 4 * q + jnp.minimum(counts[q], 3), at)
                counts[q] = counts[q] + hit.astype(I32)
            r.halo_at[b, f] = at
        return tuple(counts)

    lax.fori_loop(0, 4, rank_step, (jnp.int32(0),) * 4)


def rank_asked(r, odd, roles):
    codes = (jnp.where(odd, 1, 2), jnp.where(odd, 2, 1), 4, 3)

    def ask_step(b, state):
        state = [list(row) for row in state]
        for f in range(6):
            for i, q in enumerate(roles):
                v = r.asked_s[q, b, f]
                count = state[i][4]
                hit = lax.shift_right_arithmetic(v, 2) == codes[q]
                face = (v & 3) * 6 + (f ^ 1)
                for j in range(4):
                    state[i][j] = jnp.where(hit & (count == j), face, state[i][j])
                state[i][4] = count + hit.astype(I32)
        return tuple(tuple(row) for row in state)

    return lax.fori_loop(0, 4, ask_step, ((jnp.int32(0),) * 5,) * len(roles))


def settle(r, places):
    for j in range(4):
        mine = r.blocks[jnp.minimum(places[j], 3)].astype(F32)
        other = r.moved[jnp.maximum(places[j] - 4, 0)].astype(F32)
        block = jnp.where(places[j] < 4, mine, other)
        for x in range(8):
            rows = pl.ds(x * 32 + j * 8, 8)
            kept = jnp.where(r.mask[rows, :] > 0.5, block[8 * x : 8 * x + 8], 0.0)
            for t in range(4):
                r.nat[t, rows, :] = kept[:, 128 * t : 128 * t + 128]


def build_faces(r, recv_f):
    low = lanes_low()

    def put(number, tiles):
        face = jnp.concatenate(tiles, axis=0).astype(BF16)
        r.faces[number] = face
        recv_f[16 + number] = face

    for b in range(4):
        for f in range(2):
            put(b * 6 + f, [r.nat[t, pl.ds(7 * f * 32 + b * 8, 8), :] for t in range(4)])
            put(
                b * 6 + 2 + f,
                [r.nat[t, pl.ds(b * 8 + 7 * f, 8, stride=32), :] for t in range(4)],
            )
            face = []
            for x in range(4):
                here = r.nat[3 * f, pl.ds(x * 32 + b * 8, 8), :]
                there = r.nat[3 * f, pl.ds((x + 4) * 32 + b * 8, 8), :]
                if f == 0:
                    there = half_turn(there)
                else:
                    here = half_turn(here)
                face.append(jnp.where(low, here, there))
            put(b * 6 + 4 + f, face)


def pick_faces(r, layer, role, asked):
    for j in range(4):
        r.send_f[layer, 4 * role + j] = r.faces[asked[j]]


def read_halos(r, recv_f):
    def halo(b, f):
        both = recv_f[r.halo_at[b, f]].astype(F32)
        return [both[8 * t : 8 * t + 8] for t in range(4)]

    return [[halo(b, f) for f in range(6)] for b in range(4)]


def shifted_rows(tile):
    sub = lax.broadcasted_iota(I32, tile.shape, 0)
    return (
        jnp.where(sub == 0, 0.0, pltpu.roll(tile, 1, 0)),
        tile,
        jnp.where(sub == 7, 0.0, pltpu.roll(tile, 7, 0)),
    )


def put_pair(ref, at, row, tiles):
    ref[at + (pl.ds(row, 16), slice(None))] = jnp.concatenate(tiles, axis=0).astype(BF16)


def build_lhs(r):
    none8 = jnp.zeros((8, 128), F32)
    for x in range(8):
        for pair in range(2):
            row = x * 32 + pair * 16
            parts = []
            for b in (2 * pair, 2 * pair + 1):
                tiles = [r.nat[t, pl.ds(x * 32 + b * 8, 8), :] for t in range(4)]
                parts.append(shifted_rows(widen(tiles, none8, none8)))
            for dy in range(3):
                put_pair(r.lhs, (dy,), row, [part[dy] for part in parts])


def over_dx(three):
    rim = jnp.zeros((32, 128), F32)
    return (
        three[:, 128:256]
        + jnp.concatenate([rim, three[0:224, 0:128]], axis=0)
        + jnp.concatenate([three[32:256, 256:384], rim], axis=0)
    )


def convolve_own(r, layer):
    for k in range(4):
        window = jnp.concatenate([r.lhs[dy, :, pl.ds(128 * k, 256)] for dy in range(3)], axis=1)
        three = jnp.dot(window, r.banded[layer], preferred_element_type=F32)
        r.acc[k] = over_dx(three)


def add_halos(r, layer, halos):
    none8 = jnp.zeros((8, 128), F32)
    low = lanes_low()
    for f in range(2):
        for pair in range(2):
            wide = [widen(halos[b][f], none8, none8) for b in (2 * pair, 2 * pair + 1)]
            put_pair(r.x_lhs, (f,), 16 * pair, wide)
            wide = [widen(halos[b][2 + f], none8, none8) for b in (2 * pair, 2 * pair + 1)]
            put_pair(r.y_lhs, (f,), 16 * pair, wide)
    for pair in range(2):
        parts = [[None] * 2 for _ in range(8)]
        for i, b in enumerate((2 * pair, 2 * pair + 1)):
            for x in range(4):
                first, last = halos[b][4][x], halos[b][5][x]
                parts[x][i] = shifted_rows(jnp.where(low, first, half_turn(last)))
                parts[x + 4][i] = shifted_rows(jnp.where(low, half_turn(first), last))
        for x in range(8):
            for dy in range(3):
                put_pair(r.z_lhs, (dy,), x * 32 + 16 * pair, [part[dy] for part in parts[x]])

    def over_rows(tile):
        return (
            shifted_rows(tile[:, 0:128])[0]
            + tile[:, 128:256]
            + shifted_rows(tile[:, 256:384])[2]
        )

    for f in range(2):
        window = jnp.concatenate([r.x_lhs[f, :, pl.ds(128 * k, 256)] for k in range(4)], axis=0)
        over_dy = jnp.concatenate(
            [r.banded[layer, pl.ds(256 * dy, 256), pl.ds(256 * f, 128)] for dy in range(3)], axis=1
        )
        part = jnp.dot(window, over_dy, preferred_element_type=F32)
        for k in range(4):
            for b in range(4):
                rows = pl.ds(224 * f + 8 * b, 8)
                tile = part[32 * k + 8 * b : 32 * k + 8 * b + 8]
                r.acc[k, rows, :] = r.acc[k, rows, :] + over_rows(tile)

        window = jnp.concatenate([r.y_lhs[f, :, pl.ds(128 * k, 256)] for k in range(4)], axis=0)
        part = jnp.dot(
            window, r.banded[layer, pl.ds(512 * f, 256), :], preferred_element_type=F32
        )
        for k in range(4):
            for b in range(4):
                tile = part[32 * k + 8 * b : 32 * k + 8 * b + 8]
                r.y_add[f, k, b] = over_rows(tile)

    window = jnp.concatenate([r.z_lhs[dy] for dy in range(3)], axis=1)
    ends = jnp.concatenate(
        [r.banded[layer, pl.ds(dy * 256 + at, 64), :] for dy in range(3) for at in (0, 192)], axis=0
    )
    z_add = over_dx(jnp.dot(window, ends, preferred_element_type=F32))

    sub = lax.broadcasted_iota(I32, (8, 128), 0)
    for k in range(4):
        for x in range(8):
            for b in range(4):
                rows = pl.ds(x * 32 + b * 8, 8)
                first = jnp.broadcast_to(r.y_add[0, k, b, pl.ds(x, 1), :], (8, 128))
                last = jnp.broadcast_to(r.y_add[1, k, b, pl.ds(x, 1), :], (8, 128))
                tile = r.acc[k, rows, :]
                tile = tile + jnp.where(sub == 0, first, jnp.where(sub == 7, last, 0.0))
                side = z_add[x * 32 + b * 8 : x * 32 + b * 8 + 8]
                if k == 0:
                    tile = tile + jnp.where(low, side, 0.0)
                if k == 3:
                    tile = tile + jnp.where(low, 0.0, side)
                r.acc[k, rows, :] = tile


def finish(r, layer):
    group_lane = lax.broadcasted_iota(I32, (256, 128), 1) // 64
    group_row = lax.rem(lax.broadcasted_iota(I32, (256, 128), 0), 128) // 64
    averager = jnp.where(group_lane == group_row, 1.0 / 64.0, 0.0).astype(BF16)
    gain = r.g_v[pl.ds(layer, 1), :]
    gain = jnp.concatenate([gain, gain], axis=1)
    for k in range(4):
        total = r.acc[k]
        square = total * total
        coarse = square.astype(BF16)
        fine = (square - coarse.astype(F32)).astype(BF16)
        mean = jnp.dot(
            jnp.concatenate([coarse, fine], axis=1), averager, preferred_element_type=F32
        )
        scaled = total * lax.rsqrt(mean + 1e-5) * gain
        keep = r.mask[:, pl.ds(128 * k, 128)] > 0.5
        done = jnp.where(keep, jnp.maximum(scaled, 0.0), 0.0)
        if layer == 0:
            r.nat[k] = done
        else:
            cells = done.reshape(8, 4, 8, 128)
            for b in range(4):
                r.out[b, :, :, pl.ds(128 * k, 128)] = cells[:, b].astype(BF16)


def kernel(groups, owners, *refs):
    r = types.SimpleNamespace(**dict(zip(OPERANDS + tuple(SCRATCH), refs)))
    grp = lax.axis_index("grp")
    own = lax.axis_index("curve")
    odd = lax.rem(own, 2) == 1
    sides = (
        (grp, jnp.clip(own - 1 + 2 * lax.rem(own, 2), 0, owners - 1)),
        (grp, own + 1 - 2 * lax.rem(own, 2)),
        (jnp.maximum(grp - 1, 0), own),
        (jnp.minimum(grp + 1, groups - 1), own),
    )
    there = ((own > 0) & (own < owners - 1), own >= 0, grp > 0, grp < groups - 1)
    mirror = (0, 1, 3, 2)

    def at_side(q, step):
        if q == 1:
            step()
        else:
            pl.when(there[q])(step)

    def send(source, target, sems, q):
        return pltpu.make_async_remote_copy(
            src_ref=source,
            dst_ref=target,
            send_sem=sems[0],
            recv_sem=sems[1],
            device_id=sides[q],
            device_id_type=MESH,
        )

    barrier = pltpu.get_barrier_semaphore()
    for q in range(4):
        at_side(
            q,
            lambda: pl.semaphore_signal(
                barrier, inc=1, device_id=sides[q], device_id_type=MESH
            ),
        )
    local = [
        pltpu.make_async_copy(source, target, r.in_sems.at[i])
        for i, (source, target) in enumerate(
            (
                (r.feat, r.blocks),
                (r.swaps, r.swaps_s),
                (r.nbrs, r.nbrs_s),
                (r.occ, r.occ_v),
                (r.wts, r.w_v),
                (r.gains, r.g_v),
            )
        )
    ]
    for copy in local:
        copy.start()
    load = r.loads[0]
    tail = jnp.maximum(load - 1, 0)
    local[0].wait()
    r.outgoing[2] = r.blocks[jnp.where(odd, tail, 0)]
    r.outgoing[0] = r.blocks[jnp.where(odd, 0, jnp.maximum(load - 2, 0))]
    r.outgoing[1] = r.blocks[jnp.where(odd, 1, tail)]
    pl.semaphore_wait(barrier, sum(flag.astype(I32) for flag in there))

    cross_copy = send(
        r.outgoing.at[pl.ds(2, 1)],
        r.moved.at[pl.ds(2, 1)],
        (r.block_send.at[0], r.block_recv.at[0]),
        0,
    )
    pair_copy = send(
        r.outgoing.at[pl.ds(0, 2)],
        r.moved.at[pl.ds(0, 2)],
        (r.block_send.at[1], r.block_recv.at[1]),
        1,
    )
    lists = [
        send(
            r.nbrs,
            r.asked_s.at[mirror[q]],
            (r.list_send.at[q], r.list_recv.at[mirror[q]]),
            q,
        )
        for q in range(4)
    ]
    at_side(0, lists[0].start)
    at_side(0, cross_copy.start)
    for q in (2, 3, 1):
        at_side(q, lists[q].start)
    pair_copy.start()

    for copy in local[1:]:
        copy.wait()
    places, final = settle_places(r, owners, own, odd, load, tail)
    build_mask(r, final)
    build_weights(r)
    rank_halos(r, odd)
    for recv_f in (r.recv_first, r.recv_second):
        recv_f[40] = jnp.zeros((32, 128), BF16)
    for q in (0, 2, 3):

        @pl.when(jnp.logical_not(there[q]))
        def _():
            for b in range(4):
                for f in range(6):
                    r.asked_s[q, b, f] = -1

    for q in (1, 2, 3):
        at_side(q, lists[mirror[q]].wait_recv)
    asked = list(rank_asked(r, odd, (1, 2, 3)))
    at_side(0, lists[0].wait_recv)
    asked = list(rank_asked(r, odd, (0,))) + asked

    pair_copy.wait_recv()
    at_side(0, cross_copy.wait_recv)
    settle(r, places)

    sent = []
    for layer in range(2):
        recv_f = (r.recv_first, r.recv_second)[layer]
        build_faces(r, recv_f)
        copies = [
            send(
                r.send_f.at[layer, pl.ds(4 * q, 4)],
                recv_f.at[pl.ds(4 * mirror[q], 4)],
                (r.face_send.at[layer, q], r.face_recv.at[layer, mirror[q]]),
                q,
            )
            for q in range(4)
        ]
        for q in (0, 2, 3, 1):
            pick_faces(r, layer, q, asked[q])
            at_side(q, copies[q].start)

        build_lhs(r)
        convolve_own(r, layer)
        for q in (1, 2, 3, 0):
            at_side(q, copies[mirror[q]].wait_recv)
        add_halos(r, layer, read_halos(r, recv_f))
        finish(r, layer)
        sent += copies

    for q in range(4):
        at_side(q, lists[q].wait_send)
        at_side(q, sent[q].wait_send)
        at_side(q, sent[4 + q].wait_send)
    at_side(0, cross_copy.wait_send)
    pair_copy.wait_send()


def local_program(groups, owners, features, block_loads, swap_counts, neighbours, occupancy, conv_weights, norm_gains):
    operands = (
        features.reshape(4, 64, 512),
        swap_counts,
        neighbours,
        occupancy,
        conv_weights,
        norm_gains,
    )
    in_hbm = pl.BlockSpec(memory_space=pltpu.HBM)
    return pl.pallas_call(
        functools.partial(kernel, groups, owners),
        out_shape=jax.ShapeDtypeStruct((4, 8, 8, 512), BF16),
        in_specs=[pl.BlockSpec(memory_space=pltpu.SMEM)] + [in_hbm] * 6,
        out_specs=pl.BlockSpec(memory_space=pltpu.VMEM),
        scratch_shapes=list(SCRATCH.values()),
        compiler_params=pltpu.CompilerParams(
            collective_id=0, has_side_effects=True, vmem_limit_bytes=32 * 1024 * 1024
        ),
    )(block_loads, *[pltpu.with_memory_space_constraint(operand, pltpu.HBM) for operand in operands])


def solution(mesh):
    groups, owners = mesh.shape["grp"], mesh.shape["curve"]
    return jax.shard_map(
        functools.partial(local_program, groups, owners),
        mesh=mesh,
        in_specs=(
            P(("grp", "curve"), None, None, None),
            P(("grp", "curve")),
            P("grp", None, None),
            P(("grp", "curve"), None),
            P(("grp", "curve"), None),
            P(),
            P(),
        ),
        out_specs=P(("grp", "curve"), None, None, None),
        check_vma=False,
    )
```

```python
import functools
import types

import jax
import jax.numpy as jnp
from jax import lax
from jax.experimental import pallas as pl
from jax.experimental.pallas import tpu as pltpu
from jax.sharding import PartitionSpec as P

F32 = jnp.float32
BF16 = jnp.bfloat16
I32 = jnp.int32
MESH = pl.DeviceIdType.MESH

SCRATCH = dict(
    blocks=pltpu.VMEM((4, 64, 512), BF16),
    moved=pltpu.VMEM((2, 64, 512), BF16),
    crossed=pltpu.VMEM((1, 64, 512), BF16),
    far_occ=pltpu.VMEM((4, 512), I32),
    my_load=pltpu.VMEM((8, 128), I32),
    far_load=pltpu.VMEM((8, 128), I32),
    lent_f=pltpu.VMEM((6, 32, 128), BF16),
    lent=pltpu.VMEM((4, 64, 128), F32),
    outgoing=pltpu.VMEM((3, 64, 512), BF16),
    swaps_s=pltpu.SMEM((1, 2, 32), I32),
    nbrs_s=pltpu.SMEM((4, 6), I32),
    asked_s=pltpu.SMEM((4, 4, 6), I32),
    halo_at=pltpu.SMEM((4, 6), I32),
    occ_v=pltpu.VMEM((4, 512), I32),
    w_v=pltpu.VMEM((2, 27, 64, 64), BF16),
    g_v=pltpu.VMEM((2, 64), F32),
    banded=pltpu.VMEM((2, 768, 384), BF16),
    mask=pltpu.VMEM((256, 512), F32),
    nat=pltpu.VMEM((4, 256, 128), F32),
    faces=pltpu.VMEM((24, 32, 128), BF16),
    send_f=pltpu.VMEM((2, 16, 32, 128), BF16),
    recv_first=pltpu.VMEM((41, 32, 128), BF16),
    recv_second=pltpu.VMEM((41, 32, 128), BF16),
    lhs=pltpu.VMEM((3, 256, 640), BF16),
    x_lhs=pltpu.VMEM((2, 32, 640), BF16),
    y_lhs=pltpu.VMEM((2, 32, 640), BF16),
    z_lhs=pltpu.VMEM((3, 256, 128), BF16),
    acc=pltpu.VMEM((4, 256, 128), F32),
    y_add=pltpu.VMEM((2, 4, 4, 8, 128), F32),
    in_sems=pltpu.SemaphoreType.DMA((6,)),
    list_send=pltpu.SemaphoreType.DMA((4,)),
    list_recv=pltpu.SemaphoreType.DMA((4,)),
    block_send=pltpu.SemaphoreType.DMA((4,)),
    block_recv=pltpu.SemaphoreType.DMA((4,)),
    face_send=pltpu.SemaphoreType.DMA((2, 4)),
    face_recv=pltpu.SemaphoreType.DMA((2, 4)),
)
OPERANDS = ("loads", "feat", "swaps", "nbrs", "occ", "wts", "gains", "out")


def lanes_low():
    return lax.broadcasted_iota(I32, (8, 128), 1) < 64


def half_turn(tile):
    return pltpu.roll(tile, 64, 1)


def widen(tiles, low_side, high_side):
    low = lanes_low()
    turned = [half_turn(t) for t in tiles]
    out = [jnp.where(low, low_side, turned[0])]
    for t in range(1, 4):
        out.append(jnp.where(low, turned[t - 1], turned[t]))
    out.append(jnp.where(low, turned[3], high_side))
    return jnp.concatenate(out, axis=1)


def build_weights(r):
    zero_w = jnp.zeros((64, 64), BF16)

    @pl.loop(0, 2)
    def _(layer):
        for dx in range(3):
            for dy in range(3):
                w = [r.w_v[layer, dx * 9 + dy * 3 + dz] for dz in range(3)]
                rows = [(w[0], zero_w), (w[1], w[0]), (w[2], w[1]), (zero_w, w[2])]
                for zi in range(4):
                    r.banded[layer, pl.ds((dy * 4 + zi) * 64, 64), pl.ds(dx * 128, 128)] = (
                        jnp.concatenate(rows[zi], axis=1)
                    )


def settle_places(r, owners, own, odd, load, tail):
    swap = r.swaps_s[0, 0, own - lax.rem(own, 2)]
    flow_in = jnp.where(own > 0, r.swaps_s[0, 1, jnp.maximum(own - 1, 0)], 0)
    flow_out = jnp.where(own < owners - 1, r.swaps_s[0, 1, own], 0)
    first_load = load + jnp.where(odd, swap, -swap)
    came = jnp.maximum(flow_in, 0)
    dropped = jnp.maximum(-flow_in, 0)
    middle = first_load - dropped - jnp.maximum(flow_out, 0)
    taken = jnp.maximum(-flow_out, 0)
    final = first_load + flow_in - flow_out
    came_at = jnp.where(odd, jnp.where(swap > 0, 4, jnp.where(swap < 0, 0, 5)), 6)
    taken_at = jnp.where(odd, 6, jnp.where(swap > 0, tail, jnp.where(swap < 0, 5, 4)))
    places = []
    for j in range(4):
        i = j - came + dropped
        even_at = jnp.where(i < load - jnp.maximum(swap, 0), i, 4)
        odd_at = jnp.where((swap > 0) & (i == 0), 5, i - swap)
        kept_at = jnp.where(odd, odd_at, even_at)
        at = jnp.where(
            j < came,
            came_at,
            jnp.where(j < came + middle, kept_at, jnp.where(j < came + middle + taken, taken_at, 0)),
        )
        places.append(jnp.clip(at, 0, 6))
    return places, final


def spread_rows(occupied):
    blocks = occupied.shape[0]
    lane3 = lax.broadcasted_iota(I32, (blocks, 8, 128), 2)
    sub3 = lax.broadcasted_iota(I32, (blocks, 8, 128), 1)
    strips = []
    for x in range(8):
        strip = occupied[:, 128 * (x // 2) : 128 * (x // 2) + 128]
        wide = jnp.broadcast_to(strip[:, None, :], (blocks, 8, 128))
        pick = (lane3 // 8) == (sub3 + 8 * (x % 2))
        strips.append(jnp.where(pick, wide, 0.0).reshape(8 * blocks, 128))
    strips = jnp.concatenate(strips, axis=0).astype(BF16)
    spread = jnp.where(
        lax.rem(lax.broadcasted_iota(I32, (128, 512), 0), 8)
        == lax.broadcasted_iota(I32, (128, 512), 1) // 64,
        1.0,
        0.0,
    ).astype(BF16)
    return jnp.dot(strips, spread, preferred_element_type=F32)


def build_mask(r, final):
    block_no = lax.broadcasted_iota(I32, (4, 512), 0)
    occupied = jnp.where((block_no < final) & (r.occ_v[...] > 0), 1.0, 0.0).astype(F32)
    r.mask[...] = spread_rows(occupied)


def lent_slot(r, owners, own, odd, rows):
    flow_in = jnp.where(own > 0, r.swaps_s[0, 1, jnp.maximum(own - 1, 0)], 0)
    flow_out = jnp.where(own < owners - 1, r.swaps_s[0, 1, own], 0)
    pair_swap = r.swaps_s[0, 0, jnp.maximum(own - 2, 0)]
    pair_flow = r.swaps_s[0, 1, jnp.maximum(own - 2, 0)]
    appended = jnp.where(odd | (flow_in >= 0), 0, 1)
    first = jnp.where(odd & (flow_out > 0), 0, -1)
    far_load = r.far_load[pl.ds(0, rows), :]
    return appended * (far_load + (pair_swap + pair_flow - flow_in)) + first


def build_lent(r, slot):
    low = lanes_low()
    block_no = lax.broadcasted_iota(I32, (4, 128), 0)
    kept = [
        jnp.where((block_no == slot) & (r.far_occ[:, pl.ds(128 * t, 128)] > 0), 1.0, 0.0)
        for t in range(4)
    ]
    keep = spread_rows(jnp.concatenate(kept, axis=1).astype(F32))
    given = r.outgoing[2].astype(F32)
    for x in range(8):
        rows = [keep[32 * x + 8 * b : 32 * x + 8 * b + 8] for b in range(4)]
        block = given[8 * x : 8 * x + 8]
        block = jnp.where(rows[0] + rows[1] + rows[2] + rows[3] > 0.5, block, 0.0)
        for t in range(4):
            r.lent[t, pl.ds(8 * x, 8), :] = block[:, 128 * t : 128 * t + 128]

    def put(number, tiles):
        r.lent_f[number] = jnp.concatenate(tiles, axis=0).astype(BF16)

    for f in range(2):
        put(f, [r.lent[t, pl.ds(56 * f, 8), :] for t in range(4)])
        put(2 + f, [r.lent[t, pl.ds(7 * f, 8, stride=8), :] for t in range(4)])
        face = []
        for x in range(4):
            here = r.lent[3 * f, pl.ds(8 * x, 8), :]
            there = r.lent[3 * f, pl.ds(8 * x + 32, 8), :]
            if f == 0:
                there = half_turn(there)
            else:
                here = half_turn(here)
            face.append(jnp.where(low, here, there))
        put(4 + f, face)


def rank_halos(r, odd):
    codes = (jnp.where(odd, 2, 1), jnp.where(odd, 1, 2), 3, 4)

    def rank_step(b, counts):
        counts = list(counts)
        for f in range(6):
            v = r.nbrs_s[b, f]
            s = lax.shift_right_arithmetic(v, 2)
            at = jnp.where(s == 0, 16 + (v & 3) * 6 + (f ^ 1), 40)
            for q in range(4):
                hit = s == codes[q]
                at = jnp.where(hit, 4 * q + jnp.minimum(counts[q], 3), at)
                counts[q] = counts[q] + hit.astype(I32)
            r.halo_at[b, f] = at
        return tuple(counts)

    lax.fori_loop(0, 4, rank_step, (jnp.int32(0),) * 4)


def rank_asked(r, odd, roles):
    codes = (jnp.where(odd, 1, 2), jnp.where(odd, 2, 1), 4, 3)

    def ask_step(b, state):
        state = [list(row) for row in state]
        for f in range(6):
            for i, q in enumerate(roles):
                v = r.asked_s[q, b, f]
                count = state[i][4]
                hit = lax.shift_right_arithmetic(v, 2) == codes[q]
                face = (v & 3) * 6 + (f ^ 1)
                for j in range(4):
                    state[i][j] = jnp.where(hit & (count == j), face, state[i][j])
                state[i][4] = count + hit.astype(I32)
        return tuple(tuple(row) for row in state)

    return lax.fori_loop(0, 4, ask_step, ((jnp.int32(0),) * 5,) * len(roles))


def settle(r, places, crossed):
    for j in range(4):
        mine = r.blocks[jnp.minimum(places[j], 3)].astype(F32)
        other = r.moved[jnp.clip(places[j] - 4, 0, 1)].astype(F32)
        block = jnp.where(places[j] < 4, mine, other)
        if crossed:
            block = jnp.where(places[j] == 6, r.crossed[0].astype(F32), block)
        for x in range(8):
            rows = pl.ds(x * 32 + j * 8, 8)
            kept = jnp.where(r.mask[rows, :] > 0.5, block[8 * x : 8 * x + 8], 0.0)
            for t in range(4):
                r.nat[t, rows, :] = kept[:, 128 * t : 128 * t + 128]


def build_faces(r, recv_f):
    low = lanes_low()

    def put(number, tiles):
        face = jnp.concatenate(tiles, axis=0).astype(BF16)
        r.faces[number] = face
        recv_f[16 + number] = face

    def tile(t, row):
        return r.nat[t, pl.ds(pl.multiple_of(row, 8), 8), :]

    @pl.loop(0, 4)
    def _(b):
        for f in range(2):
            put(b * 6 + f, [tile(t, 7 * f * 32 + b * 8) for t in range(4)])
            put(
                b * 6 + 2 + f,
                [r.nat[t, pl.ds(b * 8 + 7 * f, 8, stride=32), :] for t in range(4)],
            )
            face = []
            for x in range(4):
                here = tile(3 * f, x * 32 + b * 8)
                there = tile(3 * f, (x + 4) * 32 + b * 8)
                if f == 0:
                    there = half_turn(there)
                else:
                    here = half_turn(here)
                face.append(jnp.where(low, here, there))
            put(b * 6 + 4 + f, face)


def pick_faces(r, layer, role, asked):
    for j in range(4):
        r.send_f[layer, 4 * role + j] = r.faces[asked[j]]


def read_halos(r, recv_f, odd, slot):
    def halo(b, f):
        both = recv_f[r.halo_at[b, f]].astype(F32)
        tiles = [both[8 * t : 8 * t + 8] for t in range(4)]
        if slot is not None:
            v = r.nbrs_s[b, f]
            across = lax.shift_right_arithmetic(v, 2) == jnp.where(odd, 2, 1)
            mine = slot == jnp.where(across, v & 3, -2)
            lent = r.lent_f[f ^ 1].astype(F32)
            tiles = [jnp.where(mine, lent[8 * t : 8 * t + 8], tiles[t]) for t in range(4)]
        return tiles

    return [[halo(b, f) for f in range(6)] for b in range(4)]


def shifted_rows(tile):
    sub = lax.broadcasted_iota(I32, tile.shape, 0)
    return (
        jnp.where(sub == 0, 0.0, pltpu.roll(tile, 1, 0)),
        tile,
        jnp.where(sub == 7, 0.0, pltpu.roll(tile, 7, 0)),
    )


def put_pair(ref, at, row, tiles):
    ref[at + (pl.ds(row, 16), slice(None))] = jnp.concatenate(tiles, axis=0).astype(BF16)


def build_lhs(r):
    none8 = jnp.zeros((8, 128), F32)

    @pl.loop(0, 8)
    def _(x):
        for pair in range(2):
            parts = []
            for b in (2 * pair, 2 * pair + 1):
                rows = pl.ds(pl.multiple_of(x * 32 + b * 8, 8), 8)
                tiles = [r.nat[t, rows, :] for t in range(4)]
                parts.append(shifted_rows(widen(tiles, none8, none8)))
            row = pl.multiple_of(x * 32 + pair * 16, 16)
            for dy in range(3):
                put_pair(r.lhs, (dy,), row, [part[dy] for part in parts])


def over_dx(three):
    rim = jnp.zeros((32, 128), F32)
    return (
        three[:, 128:256]
        + jnp.concatenate([rim, three[0:224, 0:128]], axis=0)
        + jnp.concatenate([three[32:256, 256:384], rim], axis=0)
    )


def convolve_own(r, layer):
    for k in range(4):
        window = jnp.concatenate([r.lhs[dy, :, pl.ds(128 * k, 256)] for dy in range(3)], axis=1)
        three = jnp.dot(window, r.banded[layer], preferred_element_type=F32)
        r.acc[k] = over_dx(three)


def add_halos(r, layer, halos):
    none8 = jnp.zeros((8, 128), F32)
    low = lanes_low()
    for f in range(2):
        for pair in range(2):
            wide = [widen(halos[b][f], none8, none8) for b in (2 * pair, 2 * pair + 1)]
            put_pair(r.x_lhs, (f,), 16 * pair, wide)
            wide = [widen(halos[b][2 + f], none8, none8) for b in (2 * pair, 2 * pair + 1)]
            put_pair(r.y_lhs, (f,), 16 * pair, wide)
    for pair in range(2):
        parts = [[None] * 2 for _ in range(8)]
        for i, b in enumerate((2 * pair, 2 * pair + 1)):
            for x in range(4):
                first, last = halos[b][4][x], halos[b][5][x]
                parts[x][i] = shifted_rows(jnp.where(low, first, half_turn(last)))
                parts[x + 4][i] = shifted_rows(jnp.where(low, half_turn(first), last))
        for x in range(8):
            for dy in range(3):
                put_pair(r.z_lhs, (dy,), x * 32 + 16 * pair, [part[dy] for part in parts[x]])

    def over_rows(tile):
        return (
            shifted_rows(tile[:, 0:128])[0]
            + tile[:, 128:256]
            + shifted_rows(tile[:, 256:384])[2]
        )

    for f in range(2):
        window = jnp.concatenate([r.x_lhs[f, :, pl.ds(128 * k, 256)] for k in range(4)], axis=0)
        over_dy = jnp.concatenate(
            [r.banded[layer, pl.ds(256 * dy, 256), pl.ds(256 * f, 128)] for dy in range(3)], axis=1
        )
        part = jnp.dot(window, over_dy, preferred_element_type=F32)
        for k in range(4):
            for b in range(4):
                rows = pl.ds(224 * f + 8 * b, 8)
                tile = part[32 * k + 8 * b : 32 * k + 8 * b + 8]
                r.acc[k, rows, :] = r.acc[k, rows, :] + over_rows(tile)

        window = jnp.concatenate([r.y_lhs[f, :, pl.ds(128 * k, 256)] for k in range(4)], axis=0)
        part = jnp.dot(
            window, r.banded[layer, pl.ds(512 * f, 256), :], preferred_element_type=F32
        )
        for k in range(4):
            for b in range(4):
                tile = part[32 * k + 8 * b : 32 * k + 8 * b + 8]
                r.y_add[f, k, b] = over_rows(tile)

    window = jnp.concatenate([r.z_lhs[dy] for dy in range(3)], axis=1)
    ends = jnp.concatenate(
        [r.banded[layer, pl.ds(dy * 256 + at, 64), :] for dy in range(3) for at in (0, 192)], axis=0
    )
    z_add = over_dx(jnp.dot(window, ends, preferred_element_type=F32))

    sub = lax.broadcasted_iota(I32, (8, 128), 0)
    for k in range(4):
        for x in range(8):
            for b in range(4):
                rows = pl.ds(x * 32 + b * 8, 8)
                first = jnp.broadcast_to(r.y_add[0, k, b, pl.ds(x, 1), :], (8, 128))
                last = jnp.broadcast_to(r.y_add[1, k, b, pl.ds(x, 1), :], (8, 128))
                tile = r.acc[k, rows, :]
                tile = tile + jnp.where(sub == 0, first, jnp.where(sub == 7, last, 0.0))
                side = z_add[x * 32 + b * 8 : x * 32 + b * 8 + 8]
                if k == 0:
                    tile = tile + jnp.where(low, side, 0.0)
                if k == 3:
                    tile = tile + jnp.where(low, 0.0, side)
                r.acc[k, rows, :] = tile


def finish(r, layer):
    group_lane = lax.broadcasted_iota(I32, (128, 128), 1) // 64
    group_row = lax.broadcasted_iota(I32, (128, 128), 0) // 64
    averager = jnp.where(group_lane == group_row, 1.0 / 64.0, 0.0).astype(BF16)
    gain = r.g_v[pl.ds(layer, 1), :]
    gain = jnp.concatenate([gain, gain], axis=1)
    squares = jnp.concatenate([(r.acc[k] * r.acc[k]).astype(BF16) for k in range(4)], axis=0)
    means = jnp.dot(squares, averager, preferred_element_type=F32)
    for k in range(4):
        scaled = r.acc[k] * lax.rsqrt(means[256 * k : 256 * k + 256] + 1e-5) * gain
        keep = r.mask[:, pl.ds(128 * k, 128)] > 0.5
        done = jnp.where(keep, jnp.maximum(scaled, 0.0), 0.0)
        if layer == 0:
            r.nat[k] = done
        else:
            cells = done.reshape(8, 4, 8, 128)
            for b in range(4):
                r.out[b, :, :, pl.ds(128 * k, 128)] = cells[:, b].astype(BF16)


def kernel(groups, owners, *refs):
    r = types.SimpleNamespace(**dict(zip(OPERANDS + tuple(SCRATCH), refs)))
    grp = lax.axis_index("grp")
    own = lax.axis_index("curve")
    odd = lax.rem(own, 2) == 1
    sides = (
        (grp, jnp.clip(own - 1 + 2 * lax.rem(own, 2), 0, owners - 1)),
        (grp, own + 1 - 2 * lax.rem(own, 2)),
        (jnp.maximum(grp - 1, 0), own),
        (jnp.minimum(grp + 1, groups - 1), own),
    )
    there = ((own > 0) & (own < owners - 1), own >= 0, grp > 0, grp < groups - 1)
    mirror = (0, 1, 3, 2)

    def at_side(q, step):
        if q == 1:
            step()
        else:
            pl.when(there[q])(step)

    def send(source, target, sems, q):
        return pltpu.make_async_remote_copy(
            src_ref=source,
            dst_ref=target,
            send_sem=sems[0],
            recv_sem=sems[1],
            device_id=sides[q],
            device_id_type=MESH,
        )

    barrier = pltpu.get_barrier_semaphore()
    for q in range(4):
        at_side(
            q,
            lambda: pl.semaphore_signal(
                barrier, inc=1, device_id=sides[q], device_id_type=MESH
            ),
        )
    local = [
        pltpu.make_async_copy(source, target, r.in_sems.at[i])
        for i, (source, target) in enumerate(
            (
                (r.feat, r.blocks),
                (r.swaps, r.swaps_s),
                (r.nbrs, r.nbrs_s),
                (r.occ, r.occ_v),
                (r.wts, r.w_v),
                (r.gains, r.g_v),
            )
        )
    ]
    for copy in local:
        copy.start()
    load = r.loads[0]
    tail = jnp.maximum(load - 1, 0)
    r.my_load[...] = jnp.zeros((8, 128), I32) + load
    local[0].wait()
    r.outgoing[2] = r.blocks[jnp.where(odd, tail, 0)]
    r.outgoing[0] = r.blocks[jnp.where(odd, 0, jnp.maximum(load - 2, 0))]
    r.outgoing[1] = r.blocks[jnp.where(odd, 1, tail)]
    pl.semaphore_wait(barrier, sum(flag.astype(I32) for flag in there))

    cross_copy = send(
        r.outgoing.at[pl.ds(2, 1)],
        r.crossed.at[pl.ds(0, 1)],
        (r.block_send.at[0], r.block_recv.at[0]),
        0,
    )
    pair_copy = send(
        r.outgoing.at[pl.ds(0, 2)],
        r.moved.at[pl.ds(0, 2)],
        (r.block_send.at[1], r.block_recv.at[1]),
        1,
    )
    lists = [
        send(
            r.nbrs,
            r.asked_s.at[mirror[q]],
            (r.list_send.at[q], r.list_recv.at[mirror[q]]),
            q,
        )
        for q in range(4)
    ]
    far = [
        send(
            source,
            target,
            (r.block_send.at[2 + i], r.block_recv.at[2 + i]),
            0,
        )
        for i, (source, target) in enumerate(((r.my_load, r.far_load), (r.occ, r.far_occ)))
    ]
    at_side(0, lists[0].start)
    at_side(0, cross_copy.start)
    for copy in far:
        at_side(0, copy.start)
    for q in (2, 3, 1):
        at_side(q, lists[q].start)
    pair_copy.start()

    for copy in local[1:]:
        copy.wait()
    places, final = settle_places(r, owners, own, odd, load, tail)
    build_mask(r, final)
    build_weights(r)
    for recv_f in (r.recv_first, r.recv_second):
        recv_f[40] = jnp.zeros((32, 128), BF16)

    @pl.when(jnp.logical_not(there[0]))
    def _():
        r.far_load[...] = jnp.zeros((8, 128), I32)
        r.far_occ[...] = jnp.zeros((4, 512), I32)

    for q in (0, 2, 3):

        @pl.when(jnp.logical_not(there[q]))
        def _():
            for b in range(4):
                for f in range(6):
                    r.asked_s[q, b, f] = -1

    for q in (1, 2, 3):
        at_side(q, lists[mirror[q]].wait_recv)
    asked = list(rank_asked(r, odd, (1, 2, 3)))

    pair_copy.wait_recv()
    settle(r, places, False)
    build_faces(r, r.recv_first)
    at_side(0, lists[0].wait_recv)
    asked = list(rank_asked(r, odd, (0,))) + asked

    sent = []
    for layer in range(2):
        recv_f = (r.recv_first, r.recv_second)[layer]
        copies = [
            send(
                r.send_f.at[layer, pl.ds(4 * q, 4)],
                recv_f.at[pl.ds(4 * mirror[q], 4)],
                (r.face_send.at[layer, q], r.face_recv.at[layer, mirror[q]]),
                q,
            )
            for q in range(4)
        ]
        if layer == 1:
            build_faces(r, recv_f)
        pick_faces(r, layer, 0, asked[0])
        at_side(0, copies[0].start)
        if layer == 0:
            at_side(0, cross_copy.wait_recv)
            settle(r, places, True)
            build_faces(r, recv_f)
        for q in (2, 3, 1):
            pick_faces(r, layer, q, asked[q])
            at_side(q, copies[q].start)

        build_lhs(r)
        convolve_own(r, layer)
        if layer == 0:
            for copy in far:
                at_side(0, copy.wait_recv)
            build_lent(r, lent_slot(r, owners, own, odd, 4))
            rank_halos(r, odd)
        for q in (1, 2, 3, 0):
            at_side(q, copies[mirror[q]].wait_recv)
        slot = lent_slot(r, owners, own, odd, 8) if layer == 0 else None
        add_halos(r, layer, read_halos(r, recv_f, odd, slot))
        finish(r, layer)
        sent += copies

    for q in range(4):
        at_side(q, lists[q].wait_send)
        at_side(q, sent[q].wait_send)
        at_side(q, sent[4 + q].wait_send)
    for copy in far + [cross_copy]:
        at_side(0, copy.wait_send)
    pair_copy.wait_send()


def local_program(groups, owners, features, block_loads, swap_counts, neighbours, occupancy, conv_weights, norm_gains):
    operands = (
        features.reshape(4, 64, 512),
        swap_counts,
        neighbours,
        occupancy,
        conv_weights,
        norm_gains,
    )
    in_hbm = pl.BlockSpec(memory_space=pltpu.HBM)
    return pl.pallas_call(
        functools.partial(kernel, groups, owners),
        out_shape=jax.ShapeDtypeStruct((4, 8, 8, 512), BF16),
        in_specs=[pl.BlockSpec(memory_space=pltpu.SMEM)] + [in_hbm] * 6,
        out_specs=pl.BlockSpec(memory_space=pltpu.VMEM),
        scratch_shapes=list(SCRATCH.values()),
        compiler_params=pltpu.CompilerParams(
            collective_id=0, has_side_effects=True, vmem_limit_bytes=32 * 1024 * 1024
        ),
    )(block_loads, *[pltpu.with_memory_space_constraint(operand, pltpu.HBM) for operand in operands])


def solution(mesh):
    groups, owners = mesh.shape["grp"], mesh.shape["curve"]
    return jax.shard_map(
        functools.partial(local_program, groups, owners),
        mesh=mesh,
        in_specs=(
            P(("grp", "curve"), None, None, None),
            P(("grp", "curve")),
            P("grp", None, None),
            P(("grp", "curve"), None),
            P(("grp", "curve"), None),
            P(),
            P(),
        ),
        out_specs=P(("grp", "curve"), None, None, None),
        check_vma=False,
    )
```

```python
import functools
import types

import jax
import jax.numpy as jnp
from jax import lax
from jax.experimental import pallas as pl
from jax.experimental.pallas import tpu as pltpu
from jax.sharding import PartitionSpec as P

F32 = jnp.float32
BF16 = jnp.bfloat16
I32 = jnp.int32
MESH = pl.DeviceIdType.MESH

SCRATCH = dict(
    blocks=pltpu.VMEM((4, 64, 512), BF16),
    moved=pltpu.VMEM((3, 64, 512), BF16),
    outgoing=pltpu.VMEM((3, 64, 512), BF16),
    swaps_s=pltpu.SMEM((1, 2, 32), I32),
    nbrs_s=pltpu.SMEM((4, 6), I32),
    asked_s=pltpu.SMEM((4, 4, 6), I32),
    halo_at=pltpu.SMEM((4, 6), I32),
    occ_v=pltpu.VMEM((4, 512), I32),
    w_v=pltpu.VMEM((2, 27, 64, 64), BF16),
    g_v=pltpu.VMEM((2, 64), F32),
    banded=pltpu.VMEM((2, 768, 384), BF16),
    mask=pltpu.VMEM((256, 512), F32),
    nat=pltpu.VMEM((4, 256, 128), F32),
    faces=pltpu.VMEM((24, 32, 128), BF16),
    send_f=pltpu.VMEM((2, 16, 32, 128), BF16),
    recv_first=pltpu.VMEM((41, 32, 128), BF16),
    recv_second=pltpu.VMEM((41, 32, 128), BF16),
    lhs=pltpu.VMEM((3, 256, 640), BF16),
    x_lhs=pltpu.VMEM((2, 32, 640), BF16),
    y_lhs=pltpu.VMEM((2, 32, 640), BF16),
    z_lhs=pltpu.VMEM((3, 256, 128), BF16),
    acc=pltpu.VMEM((4, 256, 128), F32),
    y_add=pltpu.VMEM((2, 4, 4, 8, 128), F32),
    in_sems=pltpu.SemaphoreType.DMA((6,)),
    list_send=pltpu.SemaphoreType.DMA((4,)),
    list_recv=pltpu.SemaphoreType.DMA((4,)),
    block_send=pltpu.SemaphoreType.DMA((2,)),
    block_recv=pltpu.SemaphoreType.DMA((2,)),
    face_send=pltpu.SemaphoreType.DMA((2, 4)),
    face_recv=pltpu.SemaphoreType.DMA((2, 4)),
)
OPERANDS = ("loads", "feat", "swaps", "nbrs", "occ", "wts", "gains", "out")


def lanes_low():
    return lax.broadcasted_iota(I32, (8, 128), 1) < 64


def half_turn(tile):
    return pltpu.roll(tile, 64, 1)


def widen(tiles, low_side, high_side):
    low = lanes_low()
    turned = [half_turn(t) for t in tiles]
    out = [jnp.where(low, low_side, turned[0])]
    for t in range(1, 4):
        out.append(jnp.where(low, turned[t - 1], turned[t]))
    out.append(jnp.where(low, turned[3], high_side))
    return jnp.concatenate(out, axis=1)


def build_weights(r):
    zero_w = jnp.zeros((64, 64), BF16)
    for layer in range(2):
        for dx in range(3):
            for dy in range(3):
                w = [r.w_v[layer, dx * 9 + dy * 3 + dz] for dz in range(3)]
                rows = [(w[0], zero_w), (w[1], w[0]), (w[2], w[1]), (zero_w, w[2])]
                for zi in range(4):
                    r.banded[layer, pl.ds((dy * 4 + zi) * 64, 64), pl.ds(dx * 128, 128)] = (
                        jnp.concatenate(rows[zi], axis=1)
                    )


def settle_places(r, owners, own, odd, load, tail):
    swap = r.swaps_s[0, 0, own - lax.rem(own, 2)]
    flow_in = jnp.where(own > 0, r.swaps_s[0, 1, jnp.maximum(own - 1, 0)], 0)
    flow_out = jnp.where(own < owners - 1, r.swaps_s[0, 1, own], 0)
    first_load = load + jnp.where(odd, swap, -swap)
    came = jnp.maximum(flow_in, 0)
    dropped = jnp.maximum(-flow_in, 0)
    middle = first_load - dropped - jnp.maximum(flow_out, 0)
    taken = jnp.maximum(-flow_out, 0)
    final = first_load + flow_in - flow_out
    came_at = jnp.where(odd, jnp.where(swap > 0, 4, jnp.where(swap < 0, 0, 5)), 6)
    taken_at = jnp.where(odd, 6, jnp.where(swap > 0, tail, jnp.where(swap < 0, 5, 4)))
    places = []
    for j in range(4):
        i = j - came + dropped
        even_at = jnp.where(i < load - jnp.maximum(swap, 0), i, 4)
        odd_at = jnp.where((swap > 0) & (i == 0), 5, i - swap)
        kept_at = jnp.where(odd, odd_at, even_at)
        at = jnp.where(
            j < came,
            came_at,
            jnp.where(j < came + middle, kept_at, jnp.where(j < came + middle + taken, taken_at, 0)),
        )
        places.append(jnp.clip(at, 0, 6))
    return places, final


def build_mask(r, final):
    block_no = lax.broadcasted_iota(I32, (4, 512), 0)
    occupied = jnp.where((block_no < final) & (r.occ_v[...] > 0), 1.0, 0.0).astype(F32)
    lane3 = lax.broadcasted_iota(I32, (4, 8, 128), 2)
    sub3 = lax.broadcasted_iota(I32, (4, 8, 128), 1)
    strips = []
    for x in range(8):
        strip = occupied[:, 128 * (x // 2) : 128 * (x // 2) + 128]
        wide = jnp.broadcast_to(strip[:, None, :], (4, 8, 128))
        pick = (lane3 // 8) == (sub3 + 8 * (x % 2))
        strips.append(jnp.where(pick, wide, 0.0).reshape(32, 128))
    strips = jnp.concatenate(strips, axis=0).astype(BF16)
    spread = jnp.where(
        lax.rem(lax.broadcasted_iota(I32, (128, 512), 0), 8)
        == lax.broadcasted_iota(I32, (128, 512), 1) // 64,
        1.0,
        0.0,
    ).astype(BF16)
    r.mask[...] = jnp.dot(strips, spread, preferred_element_type=F32)


def rank_halos(r, odd):
    codes = (jnp.where(odd, 2, 1), jnp.where(odd, 1, 2), 3, 4)

    def rank_step(b, counts):
        counts = list(counts)
        for f in range(6):
            v = r.nbrs_s[b, f]
            s = lax.shift_right_arithmetic(v, 2)
            at = jnp.where(s == 0, 16 + (v & 3) * 6 + (f ^ 1), 40)
            for q in range(4):
                hit = s == codes[q]
                at = jnp.where(hit, 4 * q + jnp.minimum(counts[q], 3), at)
                counts[q] = counts[q] + hit.astype(I32)
            r.halo_at[b, f] = at
        return tuple(counts)

    lax.fori_loop(0, 4, rank_step, (jnp.int32(0),) * 4)


def rank_asked(r, odd, roles):
    codes = (jnp.where(odd, 1, 2), jnp.where(odd, 2, 1), 4, 3)

    def ask_step(b, state):
        state = [list(row) for row in state]
        for f in range(6):
            for i, q in enumerate(roles):
                v = r.asked_s[q, b, f]
                count = state[i][4]
                hit = lax.shift_right_arithmetic(v, 2) == codes[q]
                face = (v & 3) * 6 + (f ^ 1)
                for j in range(4):
                    state[i][j] = jnp.where(hit & (count == j), face, state[i][j])
                state[i][4] = count + hit.astype(I32)
        return tuple(tuple(row) for row in state)

    return lax.fori_loop(0, 4, ask_step, ((jnp.int32(0),) * 5,) * len(roles))


def settle(r, places):
    for j in range(4):
        mine = r.blocks[jnp.minimum(places[j], 3)].astype(F32)
        other = r.moved[jnp.maximum(places[j] - 4, 0)].astype(F32)
        block = jnp.where(places[j] < 4, mine, other)
        for x in range(8):
            rows = pl.ds(x * 32 + j * 8, 8)
            kept = jnp.where(r.mask[rows, :] > 0.5, block[8 * x : 8 * x + 8], 0.0)
            for t in range(4):
                r.nat[t, rows, :] = kept[:, 128 * t : 128 * t + 128]


def build_faces(r, recv_f):
    low = lanes_low()

    def put(number, tiles):
        face = jnp.concatenate(tiles, axis=0).astype(BF16)
        r.faces[number] = face
        recv_f[16 + number] = face

    for b in range(4):
        for f in range(2):
            put(b * 6 + f, [r.nat[t, pl.ds(7 * f * 32 + b * 8, 8), :] for t in range(4)])
            put(
                b * 6 + 2 + f,
                [r.nat[t, pl.ds(b * 8 + 7 * f, 8, stride=32), :] for t in range(4)],
            )
            face = []
            for x in range(4):
                here = r.nat[3 * f, pl.ds(x * 32 + b * 8, 8), :]
                there = r.nat[3 * f, pl.ds((x + 4) * 32 + b * 8, 8), :]
                if f == 0:
                    there = half_turn(there)
                else:
                    here = half_turn(here)
                face.append(jnp.where(low, here, there))
            put(b * 6 + 4 + f, face)


def pick_faces(r, layer, role, asked):
    for j in range(4):
        r.send_f[layer, 4 * role + j] = r.faces[asked[j]]


def read_halos(r, recv_f):
    def halo(b, f):
        both = recv_f[r.halo_at[b, f]].astype(F32)
        return [both[8 * t : 8 * t + 8] for t in range(4)]

    return [[halo(b, f) for f in range(6)] for b in range(4)]


def shifted_rows(tile):
    sub = lax.broadcasted_iota(I32, tile.shape, 0)
    return (
        jnp.where(sub == 0, 0.0, pltpu.roll(tile, 1, 0)),
        tile,
        jnp.where(sub == 7, 0.0, pltpu.roll(tile, 7, 0)),
    )


def put_pair(ref, at, row, tiles):
    ref[at + (pl.ds(row, 16), slice(None))] = jnp.concatenate(tiles, axis=0).astype(BF16)


def build_lhs(r):
    none8 = jnp.zeros((8, 128), F32)
    for x in range(8):
        for pair in range(2):
            row = x * 32 + pair * 16
            parts = []
            for b in (2 * pair, 2 * pair + 1):
                tiles = [r.nat[t, pl.ds(x * 32 + b * 8, 8), :] for t in range(4)]
                parts.append(shifted_rows(widen(tiles, none8, none8)))
            for dy in range(3):
                put_pair(r.lhs, (dy,), row, [part[dy] for part in parts])


def over_dx(three):
    rim = jnp.zeros((32, 128), F32)
    return (
        three[:, 128:256]
        + jnp.concatenate([rim, three[0:224, 0:128]], axis=0)
        + jnp.concatenate([three[32:256, 256:384], rim], axis=0)
    )


def convolve_own(r, layer):
    for k in range(4):
        window = jnp.concatenate([r.lhs[dy, :, pl.ds(128 * k, 256)] for dy in range(3)], axis=1)
        three = jnp.dot(window, r.banded[layer], preferred_element_type=F32)
        r.acc[k] = over_dx(three)


def add_halos(r, layer, halos):
    none8 = jnp.zeros((8, 128), F32)
    low = lanes_low()
    for f in range(2):
        for pair in range(2):
            wide = [widen(halos[b][f], none8, none8) for b in (2 * pair, 2 * pair + 1)]
            put_pair(r.x_lhs, (f,), 16 * pair, wide)
            wide = [widen(halos[b][2 + f], none8, none8) for b in (2 * pair, 2 * pair + 1)]
            put_pair(r.y_lhs, (f,), 16 * pair, wide)
    for pair in range(2):
        parts = [[None] * 2 for _ in range(8)]
        for i, b in enumerate((2 * pair, 2 * pair + 1)):
            for x in range(4):
                first, last = halos[b][4][x], halos[b][5][x]
                parts[x][i] = shifted_rows(jnp.where(low, first, half_turn(last)))
                parts[x + 4][i] = shifted_rows(jnp.where(low, half_turn(first), last))
        for x in range(8):
            for dy in range(3):
                put_pair(r.z_lhs, (dy,), x * 32 + 16 * pair, [part[dy] for part in parts[x]])

    def over_rows(tile):
        return (
            shifted_rows(tile[:, 0:128])[0]
            + tile[:, 128:256]
            + shifted_rows(tile[:, 256:384])[2]
        )

    for f in range(2):
        window = jnp.concatenate([r.x_lhs[f, :, pl.ds(128 * k, 256)] for k in range(4)], axis=0)
        over_dy = jnp.concatenate(
            [r.banded[layer, pl.ds(256 * dy, 256), pl.ds(256 * f, 128)] for dy in range(3)], axis=1
        )
        part = jnp.dot(window, over_dy, preferred_element_type=F32)
        for k in range(4):
            for b in range(4):
                rows = pl.ds(224 * f + 8 * b, 8)
                tile = part[32 * k + 8 * b : 32 * k + 8 * b + 8]
                r.acc[k, rows, :] = r.acc[k, rows, :] + over_rows(tile)

        window = jnp.concatenate([r.y_lhs[f, :, pl.ds(128 * k, 256)] for k in range(4)], axis=0)
        part = jnp.dot(
            window, r.banded[layer, pl.ds(512 * f, 256), :], preferred_element_type=F32
        )
        for k in range(4):
            for b in range(4):
                tile = part[32 * k + 8 * b : 32 * k + 8 * b + 8]
                r.y_add[f, k, b] = over_rows(tile)

    window = jnp.concatenate([r.z_lhs[dy] for dy in range(3)], axis=1)
    ends = jnp.concatenate(
        [r.banded[layer, pl.ds(dy * 256 + at, 64), :] for dy in range(3) for at in (0, 192)], axis=0
    )
    z_add = over_dx(jnp.dot(window, ends, preferred_element_type=F32))

    sub = lax.broadcasted_iota(I32, (8, 128), 0)
    for k in range(4):
        for x in range(8):
            for b in range(4):
                rows = pl.ds(x * 32 + b * 8, 8)
                first = jnp.broadcast_to(r.y_add[0, k, b, pl.ds(x, 1), :], (8, 128))
                last = jnp.broadcast_to(r.y_add[1, k, b, pl.ds(x, 1), :], (8, 128))
                tile = r.acc[k, rows, :]
                tile = tile + jnp.where(sub == 0, first, jnp.where(sub == 7, last, 0.0))
                side = z_add[x * 32 + b * 8 : x * 32 + b * 8 + 8]
                if k == 0:
                    tile = tile + jnp.where(low, side, 0.0)
                if k == 3:
                    tile = tile + jnp.where(low, 0.0, side)
                r.acc[k, rows, :] = tile


def finish(r, layer):
    group_lane = lax.broadcasted_iota(I32, (256, 128), 1) // 64
    group_row = lax.rem(lax.broadcasted_iota(I32, (256, 128), 0), 128) // 64
    averager = jnp.where(group_lane == group_row, 1.0 / 64.0, 0.0).astype(BF16)
    gain = r.g_v[pl.ds(layer, 1), :]
    gain = jnp.concatenate([gain, gain], axis=1)
    parts = []
    for k in range(4):
        square = r.acc[k] * r.acc[k]
        coarse = square.astype(BF16)
        fine = (square - coarse.astype(F32)).astype(BF16)
        parts.append(jnp.concatenate([coarse, fine], axis=1))
    means = jnp.dot(jnp.concatenate(parts, axis=0), averager, preferred_element_type=F32)
    for k in range(4):
        scaled = r.acc[k] * lax.rsqrt(means[256 * k : 256 * k + 256] + 1e-5) * gain
        keep = r.mask[:, pl.ds(128 * k, 128)] > 0.5
        done = jnp.where(keep, jnp.maximum(scaled, 0.0), 0.0)
        if layer == 0:
            r.nat[k] = done
        else:
            cells = done.reshape(8, 4, 8, 128)
            for b in range(4):
                r.out[b, :, :, pl.ds(128 * k, 128)] = cells[:, b].astype(BF16)


def kernel(groups, owners, *refs):
    r = types.SimpleNamespace(**dict(zip(OPERANDS + tuple(SCRATCH), refs)))
    grp = lax.axis_index("grp")
    own = lax.axis_index("curve")
    odd = lax.rem(own, 2) == 1
    sides = (
        (grp, jnp.clip(own - 1 + 2 * lax.rem(own, 2), 0, owners - 1)),
        (grp, own + 1 - 2 * lax.rem(own, 2)),
        (jnp.maximum(grp - 1, 0), own),
        (jnp.minimum(grp + 1, groups - 1), own),
    )
    there = ((own > 0) & (own < owners - 1), own >= 0, grp > 0, grp < groups - 1)
    mirror = (0, 1, 3, 2)

    def at_side(q, step):
        if q == 1:
            step()
        else:
            pl.when(there[q])(step)

    def send(source, target, sems, q):
        return pltpu.make_async_remote_copy(
            src_ref=source,
            dst_ref=target,
            send_sem=sems[0],
            recv_sem=sems[1],
            device_id=sides[q],
            device_id_type=MESH,
        )

    barrier = pltpu.get_barrier_semaphore()
    for q in range(4):
        at_side(
            q,
            lambda: pl.semaphore_signal(
                barrier, inc=1, device_id=sides[q], device_id_type=MESH
            ),
        )
    local = [
        pltpu.make_async_copy(source, target, r.in_sems.at[i])
        for i, (source, target) in enumerate(
            (
                (r.feat, r.blocks),
                (r.swaps, r.swaps_s),
                (r.nbrs, r.nbrs_s),
                (r.occ, r.occ_v),
                (r.wts, r.w_v),
                (r.gains, r.g_v),
            )
        )
    ]
    for copy in local:
        copy.start()
    load = r.loads[0]
    tail = jnp.maximum(load - 1, 0)
    local[0].wait()
    r.outgoing[2] = r.blocks[jnp.where(odd, tail, 0)]
    r.outgoing[0] = r.blocks[jnp.where(odd, 0, jnp.maximum(load - 2, 0))]
    r.outgoing[1] = r.blocks[jnp.where(odd, 1, tail)]
    pl.semaphore_wait(barrier, sum(flag.astype(I32) for flag in there))

    cross_copy = send(
        r.outgoing.at[pl.ds(2, 1)],
        r.moved.at[pl.ds(2, 1)],
        (r.block_send.at[0], r.block_recv.at[0]),
        0,
    )
    pair_copy = send(
        r.outgoing.at[pl.ds(0, 2)],
        r.moved.at[pl.ds(0, 2)],
        (r.block_send.at[1], r.block_recv.at[1]),
        1,
    )
    lists = [
        send(
            r.nbrs,
            r.asked_s.at[mirror[q]],
            (r.list_send.at[q], r.list_recv.at[mirror[q]]),
            q,
        )
        for q in range(4)
    ]
    at_side(0, lists[0].start)
    at_side(0, cross_copy.start)
    for q in (2, 3, 1):
        at_side(q, lists[q].start)
    pair_copy.start()

    for copy in local[1:]:
        copy.wait()
    places, final = settle_places(r, owners, own, odd, load, tail)
    build_mask(r, final)
    build_weights(r)
    rank_halos(r, odd)
    for recv_f in (r.recv_first, r.recv_second):
        recv_f[40] = jnp.zeros((32, 128), BF16)
    for q in (0, 2, 3):

        @pl.when(jnp.logical_not(there[q]))
        def _():
            for b in range(4):
                for f in range(6):
                    r.asked_s[q, b, f] = -1

    for q in (1, 2, 3):
        at_side(q, lists[mirror[q]].wait_recv)
    asked = list(rank_asked(r, odd, (1, 2, 3)))
    at_side(0, lists[0].wait_recv)
    asked = list(rank_asked(r, odd, (0,))) + asked

    pair_copy.wait_recv()
    at_side(0, cross_copy.wait_recv)
    settle(r, places)

    sent = []
    for layer in range(2):
        recv_f = (r.recv_first, r.recv_second)[layer]
        build_faces(r, recv_f)
        copies = [
            send(
                r.send_f.at[layer, pl.ds(4 * q, 4)],
                recv_f.at[pl.ds(4 * mirror[q], 4)],
                (r.face_send.at[layer, q], r.face_recv.at[layer, mirror[q]]),
                q,
            )
            for q in range(4)
        ]
        for q in (0, 2, 3, 1):
            pick_faces(r, layer, q, asked[q])
            at_side(q, copies[q].start)

        build_lhs(r)
        convolve_own(r, layer)
        for q in (1, 2, 3, 0):
            at_side(q, copies[mirror[q]].wait_recv)
        add_halos(r, layer, read_halos(r, recv_f))
        finish(r, layer)
        sent += copies

    for q in range(4):
        at_side(q, lists[q].wait_send)
        at_side(q, sent[q].wait_send)
        at_side(q, sent[4 + q].wait_send)
    at_side(0, cross_copy.wait_send)
    pair_copy.wait_send()


def local_program(groups, owners, features, block_loads, swap_counts, neighbours, occupancy, conv_weights, norm_gains):
    operands = (
        features.reshape(4, 64, 512),
        swap_counts,
        neighbours,
        occupancy,
        conv_weights,
        norm_gains,
    )
    in_hbm = pl.BlockSpec(memory_space=pltpu.HBM)
    return pl.pallas_call(
        functools.partial(kernel, groups, owners),
        out_shape=jax.ShapeDtypeStruct((4, 8, 8, 512), BF16),
        in_specs=[pl.BlockSpec(memory_space=pltpu.SMEM)] + [in_hbm] * 6,
        out_specs=pl.BlockSpec(memory_space=pltpu.VMEM),
        scratch_shapes=list(SCRATCH.values()),
        compiler_params=pltpu.CompilerParams(
            collective_id=0, has_side_effects=True, vmem_limit_bytes=32 * 1024 * 1024
        ),
    )(block_loads, *[pltpu.with_memory_space_constraint(operand, pltpu.HBM) for operand in operands])


def solution(mesh):
    groups, owners = mesh.shape["grp"], mesh.shape["curve"]
    return jax.shard_map(
        functools.partial(local_program, groups, owners),
        mesh=mesh,
        in_specs=(
            P(("grp", "curve"), None, None, None),
            P(("grp", "curve")),
            P("grp", None, None),
            P(("grp", "curve"), None),
            P(("grp", "curve"), None),
            P(),
            P(),
        ),
        out_specs=P(("grp", "curve"), None, None, None),
        check_vma=False,
    )
```

```python
import functools
import types

import jax
import jax.numpy as jnp
from jax import lax
from jax.experimental import pallas as pl
from jax.experimental.pallas import tpu as pltpu
from jax.sharding import PartitionSpec as P

F32 = jnp.float32
BF16 = jnp.bfloat16
I32 = jnp.int32
MESH = pl.DeviceIdType.MESH

SCRATCH = dict(
    blocks=pltpu.VMEM((4, 64, 512), BF16),
    moved=pltpu.VMEM((3, 64, 512), BF16),
    outgoing=pltpu.VMEM((3, 64, 512), BF16),
    swaps_s=pltpu.SMEM((1, 2, 32), I32),
    nbrs_s=pltpu.SMEM((4, 6), I32),
    asked_s=pltpu.SMEM((4, 4, 6), I32),
    halo_at=pltpu.SMEM((4, 6), I32),
    occ_v=pltpu.VMEM((4, 512), I32),
    w_v=pltpu.VMEM((2, 27, 64, 64), BF16),
    g_v=pltpu.VMEM((2, 64), F32),
    banded=pltpu.VMEM((2, 768, 384), BF16),
    mask=pltpu.VMEM((256, 512), F32),
    nat=pltpu.VMEM((4, 256, 128), F32),
    faces=pltpu.VMEM((24, 32, 128), BF16),
    send_f=pltpu.VMEM((2, 16, 32, 128), BF16),
    recv_first=pltpu.VMEM((41, 32, 128), BF16),
    recv_second=pltpu.VMEM((41, 32, 128), BF16),
    lhs=pltpu.VMEM((3, 256, 640), BF16),
    x_lhs=pltpu.VMEM((2, 32, 640), BF16),
    y_lhs=pltpu.VMEM((2, 32, 640), BF16),
    z_lhs=pltpu.VMEM((3, 256, 128), BF16),
    acc=pltpu.VMEM((4, 256, 128), F32),
    y_add=pltpu.VMEM((2, 4, 4, 8, 128), F32),
    in_sems=pltpu.SemaphoreType.DMA((6,)),
    list_send=pltpu.SemaphoreType.DMA((4,)),
    list_recv=pltpu.SemaphoreType.DMA((4,)),
    block_send=pltpu.SemaphoreType.DMA((2,)),
    block_recv=pltpu.SemaphoreType.DMA((2,)),
    face_send=pltpu.SemaphoreType.DMA((2, 4)),
    face_recv=pltpu.SemaphoreType.DMA((2, 4)),
)
OPERANDS = ("loads", "feat", "swaps", "nbrs", "occ", "wts", "gains", "out")


def lanes_low():
    return lax.broadcasted_iota(I32, (8, 128), 1) < 64


def half_turn(tile):
    return pltpu.roll(tile, 64, 1)


def widen(tiles, low_side, high_side):
    low = lanes_low()
    turned = [half_turn(t) for t in tiles]
    out = [jnp.where(low, low_side, turned[0])]
    for t in range(1, 4):
        out.append(jnp.where(low, turned[t - 1], turned[t]))
    out.append(jnp.where(low, turned[3], high_side))
    return jnp.concatenate(out, axis=1)


def build_weights(r):
    zero_w = jnp.zeros((64, 64), BF16)
    for layer in range(2):
        for dx in range(3):
            for dy in range(3):
                w = [r.w_v[layer, dx * 9 + dy * 3 + dz] for dz in range(3)]
                rows = [(w[0], zero_w), (w[1], w[0]), (w[2], w[1]), (zero_w, w[2])]
                for zi in range(4):
                    r.banded[layer, pl.ds((dy * 4 + zi) * 64, 64), pl.ds(dx * 128, 128)] = (
                        jnp.concatenate(rows[zi], axis=1)
                    )


def settle_places(r, owners, own, odd, load, tail):
    swap = r.swaps_s[0, 0, own - lax.rem(own, 2)]
    flow_in = jnp.where(own > 0, r.swaps_s[0, 1, jnp.maximum(own - 1, 0)], 0)
    flow_out = jnp.where(own < owners - 1, r.swaps_s[0, 1, own], 0)
    first_load = load + jnp.where(odd, swap, -swap)
    came = jnp.maximum(flow_in, 0)
    dropped = jnp.maximum(-flow_in, 0)
    middle = first_load - dropped - jnp.maximum(flow_out, 0)
    taken = jnp.maximum(-flow_out, 0)
    final = first_load + flow_in - flow_out
    came_at = jnp.where(odd, jnp.where(swap > 0, 4, jnp.where(swap < 0, 0, 5)), 6)
    taken_at = jnp.where(odd, 6, jnp.where(swap > 0, tail, jnp.where(swap < 0, 5, 4)))
    places = []
    for j in range(4):
        i = j - came + dropped
        even_at = jnp.where(i < load - jnp.maximum(swap, 0), i, 4)
        odd_at = jnp.where((swap > 0) & (i == 0), 5, i - swap)
        kept_at = jnp.where(odd, odd_at, even_at)
        at = jnp.where(
            j < came,
            came_at,
            jnp.where(j < came + middle, kept_at, jnp.where(j < came + middle + taken, taken_at, 0)),
        )
        places.append(jnp.clip(at, 0, 6))
    return places, final


def build_mask(r, final):
    block_no = lax.broadcasted_iota(I32, (4, 512), 0)
    occupied = jnp.where((block_no < final) & (r.occ_v[...] > 0), 1.0, 0.0).astype(F32)
    lane3 = lax.broadcasted_iota(I32, (4, 8, 128), 2)
    sub3 = lax.broadcasted_iota(I32, (4, 8, 128), 1)
    strips = []
    for x in range(8):
        strip = occupied[:, 128 * (x // 2) : 128 * (x // 2) + 128]
        wide = jnp.broadcast_to(strip[:, None, :], (4, 8, 128))
        pick = (lane3 // 8) == (sub3 + 8 * (x % 2))
        strips.append(jnp.where(pick, wide, 0.0).reshape(32, 128))
    strips = jnp.concatenate(strips, axis=0).astype(BF16)
    spread = jnp.where(
        lax.rem(lax.broadcasted_iota(I32, (128, 512), 0), 8)
        == lax.broadcasted_iota(I32, (128, 512), 1) // 64,
        1.0,
        0.0,
    ).astype(BF16)
    r.mask[...] = jnp.dot(strips, spread, preferred_element_type=F32)


def rank_halos(r, odd):
    codes = (jnp.where(odd, 2, 1), jnp.where(odd, 1, 2), 3, 4)

    def rank_step(b, counts):
        counts = list(counts)
        for f in range(6):
            v = r.nbrs_s[b, f]
            s = lax.shift_right_arithmetic(v, 2)
            at = jnp.where(s == 0, 16 + (v & 3) * 6 + (f ^ 1), 40)
            for q in range(4):
                hit = s == codes[q]
                at = jnp.where(hit, 4 * q + jnp.minimum(counts[q], 3), at)
                counts[q] = counts[q] + hit.astype(I32)
            r.halo_at[b, f] = at
        return tuple(counts)

    lax.fori_loop(0, 4, rank_step, (jnp.int32(0),) * 4)


def rank_asked(r, odd, roles):
    codes = (jnp.where(odd, 1, 2), jnp.where(odd, 2, 1), 4, 3)

    def ask_step(b, state):
        state = [list(row) for row in state]
        for f in range(6):
            for i, q in enumerate(roles):
                v = r.asked_s[q, b, f]
                count = state[i][4]
                hit = lax.shift_right_arithmetic(v, 2) == codes[q]
                face = (v & 3) * 6 + (f ^ 1)
                for j in range(4):
                    state[i][j] = jnp.where(hit & (count == j), face, state[i][j])
                state[i][4] = count + hit.astype(I32)
        return tuple(tuple(row) for row in state)

    return lax.fori_loop(0, 4, ask_step, ((jnp.int32(0),) * 5,) * len(roles))


def settle(r, places):
    for j in range(4):
        mine = r.blocks[jnp.minimum(places[j], 3)].astype(F32)
        other = r.moved[jnp.maximum(places[j] - 4, 0)].astype(F32)
        block = jnp.where(places[j] < 4, mine, other)
        for x in range(8):
            rows = pl.ds(x * 32 + j * 8, 8)
            kept = jnp.where(r.mask[rows, :] > 0.5, block[8 * x : 8 * x + 8], 0.0)
            for t in range(4):
                r.nat[t, rows, :] = kept[:, 128 * t : 128 * t + 128]


def build_faces(r, recv_f):
    low = lanes_low()

    def put(number, tiles):
        face = jnp.concatenate(tiles, axis=0).astype(BF16)
        r.faces[number] = face
        recv_f[16 + number] = face

    for b in range(4):
        for f in range(2):
            put(b * 6 + f, [r.nat[t, pl.ds(7 * f * 32 + b * 8, 8), :] for t in range(4)])
            put(
                b * 6 + 2 + f,
                [r.nat[t, pl.ds(b * 8 + 7 * f, 8, stride=32), :] for t in range(4)],
            )
            face = []
            for x in range(4):
                here = r.nat[3 * f, pl.ds(x * 32 + b * 8, 8), :]
                there = r.nat[3 * f, pl.ds((x + 4) * 32 + b * 8, 8), :]
                if f == 0:
                    there = half_turn(there)
                else:
                    here = half_turn(here)
                face.append(jnp.where(low, here, there))
            put(b * 6 + 4 + f, face)


def pick_faces(r, layer, role, asked):
    for j in range(4):
        r.send_f[layer, 4 * role + j] = r.faces[asked[j]]


def read_halos(r, recv_f):
    def halo(b, f):
        both = recv_f[r.halo_at[b, f]].astype(F32)
        return [both[8 * t : 8 * t + 8] for t in range(4)]

    return [[halo(b, f) for f in range(6)] for b in range(4)]


def shifted_rows(tile):
    sub = lax.broadcasted_iota(I32, tile.shape, 0)
    return (
        jnp.where(sub == 0, 0.0, pltpu.roll(tile, 1, 0)),
        tile,
        jnp.where(sub == 7, 0.0, pltpu.roll(tile, 7, 0)),
    )


def put_pair(ref, at, row, tiles):
    ref[at + (pl.ds(row, 16), slice(None))] = jnp.concatenate(tiles, axis=0).astype(BF16)


def build_lhs(r):
    none8 = jnp.zeros((8, 128), F32)
    for x in range(8):
        for pair in range(2):
            row = x * 32 + pair * 16
            parts = []
            for b in (2 * pair, 2 * pair + 1):
                tiles = [r.nat[t, pl.ds(x * 32 + b * 8, 8), :] for t in range(4)]
                parts.append(shifted_rows(widen(tiles, none8, none8)))
            for dy in range(3):
                put_pair(r.lhs, (dy,), row, [part[dy] for part in parts])


def over_dx(three):
    rim = jnp.zeros((32, 128), F32)
    return (
        three[:, 128:256]
        + jnp.concatenate([rim, three[0:224, 0:128]], axis=0)
        + jnp.concatenate([three[32:256, 256:384], rim], axis=0)
    )


def convolve_own(r, layer):
    for k in range(4):
        window = jnp.concatenate([r.lhs[dy, :, pl.ds(128 * k, 256)] for dy in range(3)], axis=1)
        three = jnp.dot(window, r.banded[layer], preferred_element_type=F32)
        r.acc[k] = over_dx(three)


def add_halos(r, layer, halos):
    none8 = jnp.zeros((8, 128), F32)
    low = lanes_low()
    for f in range(2):
        for pair in range(2):
            wide = [widen(halos[b][f], none8, none8) for b in (2 * pair, 2 * pair + 1)]
            put_pair(r.x_lhs, (f,), 16 * pair, wide)
            wide = [widen(halos[b][2 + f], none8, none8) for b in (2 * pair, 2 * pair + 1)]
            put_pair(r.y_lhs, (f,), 16 * pair, wide)
    for pair in range(2):
        parts = [[None] * 2 for _ in range(8)]
        for i, b in enumerate((2 * pair, 2 * pair + 1)):
            for x in range(4):
                first, last = halos[b][4][x], halos[b][5][x]
                parts[x][i] = shifted_rows(jnp.where(low, first, half_turn(last)))
                parts[x + 4][i] = shifted_rows(jnp.where(low, half_turn(first), last))
        for x in range(8):
            for dy in range(3):
                put_pair(r.z_lhs, (dy,), x * 32 + 16 * pair, [part[dy] for part in parts[x]])

    def over_rows(tile):
        return (
            shifted_rows(tile[:, 0:128])[0]
            + tile[:, 128:256]
            + shifted_rows(tile[:, 256:384])[2]
        )

    for f in range(2):
        window = jnp.concatenate([r.x_lhs[f, :, pl.ds(128 * k, 256)] for k in range(4)], axis=0)
        over_dy = jnp.concatenate(
            [r.banded[layer, pl.ds(256 * dy, 256), pl.ds(256 * f, 128)] for dy in range(3)], axis=1
        )
        part = jnp.dot(window, over_dy, preferred_element_type=F32)
        for k in range(4):
            for b in range(4):
                rows = pl.ds(224 * f + 8 * b, 8)
                tile = part[32 * k + 8 * b : 32 * k + 8 * b + 8]
                r.acc[k, rows, :] = r.acc[k, rows, :] + over_rows(tile)

        window = jnp.concatenate([r.y_lhs[f, :, pl.ds(128 * k, 256)] for k in range(4)], axis=0)
        part = jnp.dot(
            window, r.banded[layer, pl.ds(512 * f, 256), :], preferred_element_type=F32
        )
        for k in range(4):
            for b in range(4):
                tile = part[32 * k + 8 * b : 32 * k + 8 * b + 8]
                r.y_add[f, k, b] = over_rows(tile)

    window = jnp.concatenate([r.z_lhs[dy] for dy in range(3)], axis=1)
    ends = jnp.concatenate(
        [r.banded[layer, pl.ds(dy * 256 + at, 64), :] for dy in range(3) for at in (0, 192)], axis=0
    )
    z_add = over_dx(jnp.dot(window, ends, preferred_element_type=F32))

    sub = lax.broadcasted_iota(I32, (8, 128), 0)
    for k in range(4):
        for x in range(8):
            for b in range(4):
                rows = pl.ds(x * 32 + b * 8, 8)
                first = jnp.broadcast_to(r.y_add[0, k, b, pl.ds(x, 1), :], (8, 128))
                last = jnp.broadcast_to(r.y_add[1, k, b, pl.ds(x, 1), :], (8, 128))
                tile = r.acc[k, rows, :]
                tile = tile + jnp.where(sub == 0, first, jnp.where(sub == 7, last, 0.0))
                side = z_add[x * 32 + b * 8 : x * 32 + b * 8 + 8]
                if k == 0:
                    tile = tile + jnp.where(low, side, 0.0)
                if k == 3:
                    tile = tile + jnp.where(low, 0.0, side)
                r.acc[k, rows, :] = tile


def finish(r, layer):
    group_lane = lax.broadcasted_iota(I32, (256, 128), 1) // 64
    group_row = lax.rem(lax.broadcasted_iota(I32, (256, 128), 0), 128) // 64
    averager = jnp.where(group_lane == group_row, 1.0 / 64.0, 0.0).astype(BF16)
    gain = r.g_v[pl.ds(layer, 1), :]
    gain = jnp.concatenate([gain, gain], axis=1)
    parts = []
    for k in range(4):
        square = r.acc[k] * r.acc[k]
        coarse = square.astype(BF16)
        fine = (square - coarse.astype(F32)).astype(BF16)
        parts.append(jnp.concatenate([coarse, fine], axis=1))
    means = jnp.dot(jnp.concatenate(parts, axis=0), averager, preferred_element_type=F32)
    for k in range(4):
        scaled = r.acc[k] * lax.rsqrt(means[256 * k : 256 * k + 256] + 1e-5) * gain
        keep = r.mask[:, pl.ds(128 * k, 128)] > 0.5
        done = jnp.where(keep, jnp.maximum(scaled, 0.0), 0.0)
        if layer == 0:
            r.nat[k] = done
        else:
            cells = done.reshape(8, 4, 8, 128)
            for b in range(4):
                r.out[b, :, :, pl.ds(128 * k, 128)] = cells[:, b].astype(BF16)


def kernel(groups, owners, *refs):
    r = types.SimpleNamespace(**dict(zip(OPERANDS + tuple(SCRATCH), refs)))
    grp = lax.axis_index("grp")
    own = lax.axis_index("curve")
    odd = lax.rem(own, 2) == 1
    sides = (
        (grp, jnp.clip(own - 1 + 2 * lax.rem(own, 2), 0, owners - 1)),
        (grp, own + 1 - 2 * lax.rem(own, 2)),
        (jnp.maximum(grp - 1, 0), own),
        (jnp.minimum(grp + 1, groups - 1), own),
    )
    there = ((own > 0) & (own < owners - 1), own >= 0, grp > 0, grp < groups - 1)
    mirror = (0, 1, 3, 2)

    def at_side(q, step):
        if q == 1:
            step()
        else:
            pl.when(there[q])(step)

    def send(source, target, sems, q):
        return pltpu.make_async_remote_copy(
            src_ref=source,
            dst_ref=target,
            send_sem=sems[0],
            recv_sem=sems[1],
            device_id=sides[q],
            device_id_type=MESH,
        )

    barrier = pltpu.get_barrier_semaphore()
    for q in range(4):
        at_side(
            q,
            lambda: pl.semaphore_signal(
                barrier, inc=1, device_id=sides[q], device_id_type=MESH
            ),
        )
    local = [
        pltpu.make_async_copy(source, target, r.in_sems.at[i])
        for i, (source, target) in enumerate(
            (
                (r.feat, r.blocks),
                (r.swaps, r.swaps_s),
                (r.nbrs, r.nbrs_s),
                (r.occ, r.occ_v),
                (r.wts, r.w_v),
                (r.gains, r.g_v),
            )
        )
    ]
    for copy in local[:3]:
        copy.start()
    load = r.loads[0]
    tail = jnp.maximum(load - 1, 0)
    local[0].wait()
    r.outgoing[2] = r.blocks[jnp.where(odd, tail, 0)]
    r.outgoing[0] = r.blocks[jnp.where(odd, 0, jnp.maximum(load - 2, 0))]
    r.outgoing[1] = r.blocks[jnp.where(odd, 1, tail)]
    pl.semaphore_wait(barrier, sum(flag.astype(I32) for flag in there))

    cross_copy = send(
        r.outgoing.at[pl.ds(2, 1)],
        r.moved.at[pl.ds(2, 1)],
        (r.block_send.at[0], r.block_recv.at[0]),
        0,
    )
    pair_copy = send(
        r.outgoing.at[pl.ds(0, 2)],
        r.moved.at[pl.ds(0, 2)],
        (r.block_send.at[1], r.block_recv.at[1]),
        1,
    )
    lists = [
        send(
            r.nbrs,
            r.asked_s.at[mirror[q]],
            (r.list_send.at[q], r.list_recv.at[mirror[q]]),
            q,
        )
        for q in range(4)
    ]
    at_side(0, lists[0].start)
    at_side(0, cross_copy.start)
    for q in (2, 3, 1):
        at_side(q, lists[q].start)
    pair_copy.start()
    for copy in local[3:]:
        copy.start()

    for copy in local[1:]:
        copy.wait()
    places, final = settle_places(r, owners, own, odd, load, tail)
    build_mask(r, final)
    build_weights(r)
    rank_halos(r, odd)
    for recv_f in (r.recv_first, r.recv_second):
        recv_f[40] = jnp.zeros((32, 128), BF16)
    for q in (0, 2, 3):

        @pl.when(jnp.logical_not(there[q]))
        def _():
            for b in range(4):
                for f in range(6):
                    r.asked_s[q, b, f] = -1

    for q in (1, 2, 3):
        at_side(q, lists[mirror[q]].wait_recv)
    asked = list(rank_asked(r, odd, (1, 2, 3)))
    at_side(0, lists[0].wait_recv)
    asked = list(rank_asked(r, odd, (0,))) + asked

    pair_copy.wait_recv()
    at_side(0, cross_copy.wait_recv)
    settle(r, places)

    sent = []
    for layer in range(2):
        recv_f = (r.recv_first, r.recv_second)[layer]
        build_faces(r, recv_f)
        copies = [
            send(
                r.send_f.at[layer, pl.ds(4 * q, 4)],
                recv_f.at[pl.ds(4 * mirror[q], 4)],
                (r.face_send.at[layer, q], r.face_recv.at[layer, mirror[q]]),
                q,
            )
            for q in range(4)
        ]
        for q in (0, 2, 3, 1):
            pick_faces(r, layer, q, asked[q])
            at_side(q, copies[q].start)

        build_lhs(r)
        convolve_own(r, layer)
        for q in (1, 2, 3, 0):
            at_side(q, copies[mirror[q]].wait_recv)
        add_halos(r, layer, read_halos(r, recv_f))
        finish(r, layer)
        sent += copies

    for q in range(4):
        at_side(q, lists[q].wait_send)
        at_side(q, sent[q].wait_send)
        at_side(q, sent[4 + q].wait_send)
    at_side(0, cross_copy.wait_send)
    pair_copy.wait_send()


def local_program(groups, owners, features, block_loads, swap_counts, neighbours, occupancy, conv_weights, norm_gains):
    operands = (
        features.reshape(4, 64, 512),
        swap_counts,
        neighbours,
        occupancy,
        conv_weights,
        norm_gains,
    )
    in_hbm = pl.BlockSpec(memory_space=pltpu.HBM)
    return pl.pallas_call(
        functools.partial(kernel, groups, owners),
        out_shape=jax.ShapeDtypeStruct((4, 8, 8, 512), BF16),
        in_specs=[pl.BlockSpec(memory_space=pltpu.SMEM)] + [in_hbm] * 6,
        out_specs=pl.BlockSpec(memory_space=pltpu.VMEM),
        scratch_shapes=list(SCRATCH.values()),
        compiler_params=pltpu.CompilerParams(
            collective_id=0, has_side_effects=True, vmem_limit_bytes=32 * 1024 * 1024
        ),
    )(block_loads, *[pltpu.with_memory_space_constraint(operand, pltpu.HBM) for operand in operands])


def solution(mesh):
    groups, owners = mesh.shape["grp"], mesh.shape["curve"]
    return jax.shard_map(
        functools.partial(local_program, groups, owners),
        mesh=mesh,
        in_specs=(
            P(("grp", "curve"), None, None, None),
            P(("grp", "curve")),
            P("grp", None, None),
            P(("grp", "curve"), None),
            P(("grp", "curve"), None),
            P(),
            P(),
        ),
        out_specs=P(("grp", "curve"), None, None, None),
        check_vma=False,
    )
```
